256 devices in a mesh: gx: 32 (over y, x, core), gy: 8 (over z).
Axes of the slice: x: 4, y: 4, z: 8, core: 2. Of those that a mesh axis runs over, the one named last changes fastest.
Arguments:
- position: float32 [3, 524288], P(None, ('gx', 'gy')), may hold values from -0.5 to 0.5
- velocity: float32 [3, 524288], P(None, ('gx', 'gy')), may hold values from -6 to 6
- cell_list: int32 [4, 256, 256, 16], P(None, 'gx', 'gy'), may hold values from 0 to 2048, as said below
- slot_weight: float32 [4, 256, 256, 16], P(None, 'gx', 'gy'), may hold values from 0.25 to 1
- particle_cell: int32 [524288], P(('gx', 'gy')), may hold values from 0 to 4095, as said below
- destination: int32 [524288, 1], P(('gx', 'gy')), may hold values from 0 to 8; in each aligned block of 2048 rows (0 to 2047, 2048 to 4095, ...) at most 512 rows name the same one
- lift: float32 [32, 4], replicated, may hold values from -3 to 3
- kernel_0a: bfloat16 [27, 32, 32], replicated, may hold values from -0.4375 to 0.4375
- kernel_1a: bfloat16 [27, 32, 32], replicated, may hold values from -0.4375 to 0.4375
- kernel_2: bfloat16 [27, 32, 32], replicated, may hold values from -0.4375 to 0.4375
- kernel_1b: bfloat16 [27, 32, 32], replicated, may hold values from -0.4375 to 0.4375
- kernel_0b: bfloat16 [27, 32, 32], replicated, may hold values from -0.4375 to 0.4375
- head: bfloat16 [3, 32], replicated, may hold values from -1 to 1
Outputs:
- moved_state: float32 [6, 1179648], P(None, ('gx', 'gy'))
The draws below stay inside these ranges and needn't reach their ends.
Inputs may be any that keep to these rules, and one draw needn't show every extreme that they name: `cell_list`: on each device every local particle index below 2048 stands in exactly one slot of the device's cells, and 2048 marks an empty slot. `particle_cell`: the local cell in whose slots the particle stands. `destination`: direction 3 (a+1) + (b+1) means the device a steps along gx and b along gy, periodic; among the particles of one device at most 512 share a direction.
All inputs are finite; a program needn't handle non-finite values.
Results may differ from the reference program's by a relative error of at most 0.034.
Values may be sent and summed in bfloat16 or wider, within the bound.
No kernel may reach another device: no remote copies, remote signals or barrier semaphores. Data moves between devices by JAX's collectives and lax.ppermute only.
A program may use at most 128 MiB of HBM per device.

```python
import math
import jax
import jax.numpy as jnp
import numpy as np
from jax import lax

C = 32
SLOTS = 4
CX = 8
CY = 32
NZ = 16
NX = 256
NY = 256
CELLS_DEV = 4096
P_DEV = 2048
CAP = 512
P_ALL = 524288
N_GX = 32
N_GY = 8


def particle_layout(key):
    devices = NX // CX * (NY // CY)
    keys = jax.random.split(jax.random.fold_in(key, 11), devices)
    return jax.vmap(lambda single: jax.random.permutation(single, CELLS_DEV * SLOTS))(keys).astype(jnp.int32)


def draw_cell_list(key, part):
    orders = particle_layout(key)
    inverse = jnp.argsort(orders, axis=1, stable=True).astype(jnp.int32)
    entries = jnp.where(inverse < P_DEV, inverse, P_DEV).astype(jnp.int32)
    count_x = NX // CX
    count_y = NY // CY
    entries = entries.reshape(count_x, count_y, CELLS_DEV, SLOTS).transpose(3, 0, 1, 2)
    entries = entries.reshape(SLOTS, count_x, count_y, CX, CY, NZ).transpose(0, 1, 3, 2, 4, 5)
    return entries.reshape(SLOTS, NX, NY, NZ)


def draw_particle_cell(key, part):
    orders = particle_layout(key)
    return (orders[:, :P_DEV] // SLOTS).reshape(-1).astype(jnp.int32)


def shard_levels(stream_key, dims, cuts, least, largest):
    def one(dim, shards_of):
        draws = jax.random.uniform(jax.random.fold_in(jax.random.fold_in(stream_key, 6), dim), (shards_of,), jnp.float32, least / len(cuts), largest / len(cuts))
        return jnp.repeat(jnp.exp(draws), dims[dim] // shards_of).reshape((-1,) + (1,) * (len(dims) - dim - 1))

    loudness = one(*cuts[0])
    for cut in cuts[1:]:
        loudness = loudness * one(*cut)
    return loudness


def routed_block(rng, own, number, rows, number_of, top, bound, slope):
    sequence = jax.random.permutation(rng, number_of)
    heavy_load, ordinary = shares(number_of, rows * top, bound, slope, True), shares(number_of, rows * top, bound, slope, False)
    places = jnp.arange(number_of)

    def named(sizes, offset_by):
        used = int((sizes > 0).sum())
        fixed = max(1, used // 4)
        shifted = fixed + (places - fixed + offset_by * (used - fixed)) % max(1, number_of - fixed)
        return jnp.zeros((number_of,), jnp.int32).at[sequence[jnp.where(places < fixed, places, shifted)]].set(jnp.asarray(sizes, jnp.int32))

    sizes = jnp.where(number % 4 == 0, named(heavy_load, number // 4), named(ordinary, number - number // 4 - 1))
    mixed = jax.random.permutation(jax.random.fold_in(own, 3), number_of)
    donor, receiver = mixed[0:number_of // 2 * 2:2], mixed[1:number_of // 2 * 2:2]
    room = jnp.minimum(sizes[donor] - 1, bound - sizes[receiver]) // 2
    room = jnp.where((donor == sequence[0]) | (receiver == sequence[0]) | (sizes[receiver] == 0), 0, jnp.maximum(room, 0))
    shifted = jax.random.randint(jax.random.fold_in(own, 4), (number_of // 2,), 0, 1 << 20) % (room + 1)
    sizes = sizes.at[donor].add(-shifted).at[receiver].add(shifted)
    items = jnp.searchsorted(jnp.cumsum(sizes), jnp.arange(rows * top), side="right").astype(jnp.int32)
    table = items.reshape(top, rows).T
    table = table[jax.random.permutation(jax.random.fold_in(own, 1), rows)]
    offset_by = jax.random.randint(jax.random.fold_in(own, 2), (rows, 1), 0, top)
    return jnp.take_along_axis(table, (jnp.arange(top)[None, :] + offset_by) % top, axis=1)


def shares(count, total, most, skew, full):
    weights = [(1 << 20) // math.isqrt(standing ** skew) + 1 for standing in range(1, count + 1)]
    largest = most if full else min(most, max(-(-total // count), total * weights[0] // sum(weights)))
    least = 1 if total - largest >= count - 1 else 0
    counts, rest = [largest] + [least] * (count - 1), total - largest - least * (count - 1)
    while rest > 0:
        movable = [i for i in range(1, count) if counts[i] < largest] or [i for i in range(1, count) if counts[i] < most]
        whole, left = sum([weights[i] for i in movable]), rest
        for i in movable:
            extra = min(most - counts[i], max(1, left * weights[i] // whole), rest)
            counts[i] = counts[i] + extra
            rest = rest - extra
    return np.array(counts)


def bell_draw(stream_key, shape, scale, reach, shards=(), held_as=jnp.bfloat16):
    level = shard_levels(stream_key, shape, shards, -0.22, 0.18) if shards else 1.0
    drawn = jax.random.normal(stream_key, shape, jnp.float32) * scale * level
    return jnp.minimum(jnp.maximum(drawn, -reach), reach).astype(held_as)


def setup_inputs(seed: int = 0) -> dict:
    key_of = jax.random.split(jax.random.key(seed), 14)
    position = jnp.clip(jax.random.uniform(key_of[0], (3, P_ALL), jnp.float32, -0.5, 0.5) * shard_levels(key_of[0], (3, P_ALL), ((1, 256),), -0.4, 0.0), -0.5, 0.5)
    velocity = bell_draw(key_of[1], (3, P_ALL), 1.0, 6.0, ((1, 256),), jnp.float32)
    cell_list = draw_cell_list(jax.random.fold_in(key_of[13], 71), 0)
    slot_weight = jnp.clip(jnp.exp(math.log(1.0) - 1.3862944 * jax.random.uniform(key_of[3], (SLOTS, NX, NY, NZ), jnp.float32) ** shard_levels(key_of[3], (SLOTS, NX, NY, NZ), ((1, 32), (2, 8)), -0.2, 0.2)), 0.25, 1.0)
    particle_cell = draw_particle_cell(jax.random.fold_in(key_of[13], 71), 0)
    destination_keys = jax.random.split(jax.random.fold_in(key_of[5], 1), P_ALL // P_DEV)
    destination_turns = jax.random.permutation(jax.random.fold_in(key_of[5], 3), P_ALL // P_DEV)
    destination = jax.vmap(lambda own, number: routed_block(jax.random.fold_in(key_of[5], 2), own, number, P_DEV, 9, 1, CAP, 2))(destination_keys, destination_turns).reshape((P_ALL, 1))
    lift = bell_draw(key_of[6], (C, 4), 4 ** -0.5, 3.0, (), jnp.float32)
    kernel_0a = bell_draw(key_of[7], (27, C, C), (27 * C // 4) ** -0.5, 0.4375)
    kernel_1a = bell_draw(key_of[8], (27, C, C), (27 * C // 4) ** -0.5, 0.4375)
    kernel_2 = bell_draw(key_of[9], (27, C, C), (27 * C // 4) ** -0.5, 0.4375)
    kernel_1b = bell_draw(key_of[10], (27, C, C), (27 * C // 4) ** -0.5, 0.4375)
    kernel_0b = bell_draw(key_of[11], (27, C, C), (27 * C // 4) ** -0.5, 0.4375)
    head = bell_draw(key_of[12], (3, C), C ** -0.5, 1.0)
    return {"position": position, "velocity": velocity, "cell_list": cell_list, "slot_weight": slot_weight, "particle_cell": particle_cell, "destination": destination, "lift": lift, "kernel_0a": kernel_0a, "kernel_1a": kernel_1a, "kernel_2": kernel_2, "kernel_1b": kernel_1b, "kernel_0b": kernel_0b, "head": head}


drift_step = 0.25


def convolve(field, kernel):
    channels = kernel.shape[1]
    extent = field.shape[1]
    slab_cells = math.gcd(extent, 8)
    padded = jnp.pad(field, ((0, 0), (1, 1), (1, 1), (1, 1)), mode="wrap")
    weights = kernel.astype(jnp.float32).reshape(3, 3, 3, channels, field.shape[0]).transpose(3, 4, 0, 1, 2)

    def per_slab(start):
        piece = lax.dynamic_slice_in_dim(padded, start, slab_cells + 2, 1).astype(jnp.float32)
        result = lax.conv_general_dilated(piece[None], weights, (1, 1, 1), "VALID", dimension_numbers=("NCDHW", "OIDHW", "NCDHW"), precision=lax.Precision.HIGHEST)
        return jax.nn.gelu(result[0]).astype(jnp.bfloat16)

    starts = jnp.arange(extent // slab_cells, dtype=jnp.int32) * slab_cells
    pieces = lax.map(per_slab, starts)
    return pieces.transpose(1, 0, 2, 3, 4).reshape(channels, extent, field.shape[2], field.shape[3])


def coarsen(field):
    chans, ext_x, ext_y, ext_z = field.shape
    blocks = field.astype(jnp.float32).reshape(chans, ext_x // 2, 2, ext_y // 2, 2, ext_z // 2, 2)
    return jnp.mean(blocks, axis=(2, 4, 6)).astype(jnp.bfloat16)


def refine(field):
    return jnp.repeat(jnp.repeat(jnp.repeat(field, 2, axis=1), 2, axis=2), 2, axis=3)


def combine(fine, coarse):
    return (fine.astype(jnp.float32) + refine(coarse).astype(jnp.float32)).astype(jnp.bfloat16)


def lift_sum(lift, deposit_grid):
    total = lift[:, 0:1] * deposit_grid[0:1]
    for index in range(1, 4):
        total = total + lift[:, index:index + 1] * deposit_grid[index:index + 1]
    return total.astype(jnp.bfloat16)


def reference(position, velocity, cell_list, slot_weight, particle_cell, destination, lift, kernel_0a, kernel_1a, kernel_2, kernel_1b, kernel_0b, head):
    groups = N_GX * N_GY
    slot_lists = cell_list.reshape(SLOTS, N_GX, CX, N_GY, CY, NZ).transpose(1, 3, 0, 2, 4, 5).reshape(groups, SLOTS, CELLS_DEV)
    slot_wts = slot_weight.reshape(SLOTS, N_GX, CX, N_GY, CY, NZ).transpose(1, 3, 0, 2, 4, 5).reshape(groups, SLOTS, CELLS_DEV)
    device_vel = velocity.reshape(3, groups, P_DEV).transpose(1, 0, 2)

    def deposit(packed):
        entries, weights, speeds = packed
        lookup_table = jnp.concatenate([jnp.ones((1, P_DEV), jnp.float32), speeds], axis=0)
        lookup_table = jnp.concatenate([lookup_table, jnp.zeros((4, 1), jnp.float32)], axis=1)
        picked = jnp.take(lookup_table, entries.reshape(-1), axis=1).reshape(4, SLOTS, CELLS_DEV)
        return jnp.sum(picked * weights[None], axis=1)

    deposit_dev = lax.map(deposit, (slot_lists, slot_wts, device_vel))
    deposit_grid = deposit_dev.reshape(N_GX, N_GY, 4, CX, CY, NZ).transpose(2, 0, 3, 1, 4, 5).reshape(4, NX * NY * NZ)
    lifted = lift_sum(lift, deposit_grid).reshape(C, NX, NY, NZ)
    level_e0 = convolve(lifted, kernel_0a)
    level_e1 = convolve(coarsen(level_e0), kernel_1a)
    level_e2 = convolve(coarsen(level_e1), kernel_2)
    level_f1 = convolve(combine(level_e1, level_e2), kernel_1b)
    level_f0 = convolve(combine(level_e0, level_f1), kernel_0b)
    change = jnp.dot(head, level_f0.reshape(C, -1), preferred_element_type=jnp.float32)
    change = change.reshape(3, N_GX, CX, N_GY, CY, NZ).transpose(1, 3, 0, 2, 4, 5).reshape(groups, 3, CELLS_DEV)
    cell_ids = jnp.broadcast_to(particle_cell.reshape(groups, 1, P_DEV), (groups, 3, P_DEV))
    kick = jnp.take_along_axis(change, cell_ids, axis=2).transpose(1, 0, 2).reshape(3, P_ALL)
    new_velocity = velocity + kick
    new_position = position + drift_step * new_velocity
    payload = jnp.concatenate([new_position, new_velocity], axis=0).reshape(6, groups, P_DEV).transpose(1, 0, 2)
    headings = destination.reshape(groups, P_DEV)

    def pack(packed):
        cargo, heading = packed
        onehot = (heading[None, :] == jnp.arange(9, dtype=jnp.int32)[:, None]).astype(jnp.int32)
        arrival = jnp.sum(jnp.cumsum(onehot, axis=1) * onehot, axis=0) - 1
        slot_index = heading * CAP + arrival
        return jnp.zeros((6, 9 * CAP), cargo.dtype).at[:, slot_index].set(cargo)

    outgoing = lax.map(pack, (payload, headings)).reshape(N_GX, N_GY, 6, 3, 3, CAP)
    columns = []
    for offset_x in (-1, 0, 1):
        rows_out = []
        for offset_y in (-1, 0, 1):
            rows_out.append(jnp.roll(outgoing[:, :, :, offset_x + 1, offset_y + 1], (offset_x, offset_y), axis=(0, 1)))
        columns.append(jnp.stack(rows_out, axis=3))
    inbox = jnp.stack(columns, axis=3)
    return inbox.transpose(2, 0, 1, 3, 4, 5).reshape(6, -1)
```

```python
import jax
import jax.numpy as jnp
import numpy as np
from jax import lax
from jax.experimental import pallas as pl
from jax.experimental.pallas import tpu as pltpu
from jax.sharding import PartitionSpec as P

f32 = jnp.float32
bf16 = jnp.bfloat16
i32 = jnp.int32

CAP = 512
DRIFT = 0.25
CH = 32
NZ = 16
COLS = 28
ROWS = 32


def iota(shape, dim):
    return lax.broadcasted_iota(i32, shape, dim)


def dot(a, b):
    return jnp.dot(a, b, preferred_element_type=f32)


def gelu(x):
    inner = x * (0.7978845608028654 + 0.035677408136300125 * (x * x))
    return (0.5 * x) * (1.0 + jnp.tanh(inner))


def deposit_kernel(vel_ref, cells_ref, weight_ref, out_ref, stage):
    totals = [jnp.zeros((32, 128), f32) for _ in range(4)]
    for s in range(4):
        entry = jnp.concatenate([cells_ref[s, x] for x in range(8)], axis=1)
        weight = jnp.concatenate([weight_ref[s, x] for x in range(8)], axis=1)
        lane = jnp.bitwise_and(entry, 127)
        row = jnp.right_shift(entry, 7)
        picked = [jnp.zeros((32, 128), f32) for _ in range(3)]
        for r in range(16):
            here = row == r
            for q in range(3):
                table = jnp.broadcast_to(vel_ref[q : q + 1, r * 128 : (r + 1) * 128], (32, 128))
                got = jnp.take_along_axis(table, lane, axis=1)
                picked[q] = jnp.where(here, got, picked[q])
        totals[0] = totals[0] + jnp.where(entry < 2048, weight, 0.0)
        for q in range(3):
            totals[q + 1] = totals[q + 1] + weight * picked[q]
    group = iota((32, 128), 1) // 16
    for t in range(4):
        piece = jnp.zeros((32, 128), f32)
        for half in range(2):
            for q in range(4):
                source, target = (2 * t + half) * 16, half * 64 + q * 16
                shift = (target - source) % 128
                moved = pltpu.roll(totals[q], shift, 1) if shift else totals[q]
                piece = jnp.where(group == half * 4 + q, moved, piece)
        stage[t * 32 : t * 32 + 32, :] = piece
    for t in range(4):
        lanes = slice(t * 128, (t + 1) * 128)
        for parity in range(2):
            out_ref[parity * 16 : parity * 16 + 16, lanes] = stage[
                pl.ds(t * 32 + parity, 16, stride=2), :
            ].astype(bf16)


def deposit(velocity, cells, weight):
    return pl.pallas_call(
        deposit_kernel,
        out_shape=jax.ShapeDtypeStruct((32, 512), bf16),
        scratch_shapes=[pltpu.VMEM((128, 128), f32)],
        cost_estimate=pl.CostEstimate(flops=2_000_000, bytes_accessed=1_000_000, transcendentals=0),
    )(velocity, cells, weight)


def prep_kernel(
    first_ref, taps_ref, dest_ref, w0a_ref, w1a_ref, w2_ref, w1b_ref, w0b_ref, rank_ref
):
    row = iota((16, 128), 0)
    masks = []
    for t in range(4):
        diff = jnp.bitwise_and(row - (4 * t + iota((16, 128), 1) // 32), 15)
        masks.append((diff == 15, diff == 0, diff == 1))
    for ox in range(3):
        for oy in range(3):
            for q in range(4):
                at = (9 * ox + 3 * oy) * 4 + q
                low = jnp.broadcast_to(first_ref[at : at + 1, :], (16, 128))
                mid = jnp.broadcast_to(first_ref[at + 4 : at + 5, :], (16, 128))
                high = jnp.broadcast_to(first_ref[at + 8 : at + 9, :], (16, 128))
                for t in range(4):
                    below, same, above = masks[t]
                    piece = jnp.where(
                        same, mid, jnp.where(below, low, jnp.where(above, high, 0.0))
                    )
                    begin = oy * 256 + ox * 64 + q * 16
                    w0a_ref[begin : begin + 16, t * 128 : (t + 1) * 128] = piece.astype(bf16)
    for oy in range(3):
        w0a_ref[oy * 256 + 192 : oy * 256 + 256, :] = jnp.zeros((64, 512), bf16)

    group = iota((32, 128), 1) // 32

    def bands(number, out_ref, depth):
        tiles = depth // 4

        def one(tap, carry):
            at = number * 27 + 3 * tap
            low = taps_ref[at].astype(f32)
            mid = taps_ref[at + 1].astype(f32)
            high = taps_ref[at + 2].astype(f32)
            zero = jnp.zeros((32, 128), f32)

            def pick(*wanted):
                value = zero
                for index, piece in wanted:
                    value = jnp.where(group == index, piece, value)
                return value

            patterns = (
                {0: pick((0, mid), (1, low)), -1: pick((3, high))},
                {0: pick((0, high), (1, mid), (2, low))},
                {0: pick((1, high), (2, mid), (3, low))},
                {0: pick((2, high), (3, mid)), 1: pick((0, low))},
            )
            for z in range(depth):
                content = {}
                for step, piece in patterns[z % 4].items():
                    tile = (z // 4 + step) % tiles
                    content[tile] = content[tile] + piece if tile in content else piece
                for tile in range(tiles):
                    out_ref[tap, z * 32 : (z + 1) * 32, tile * 128 : (tile + 1) * 128] = (
                        content.get(tile, zero).astype(bf16)
                    )
            return carry

        lax.fori_loop(0, 9, one, 0)

    bands(0, w1a_ref, 8)
    bands(1, w2_ref, 4)
    bands(2, w1b_ref, 8)
    bands(3, w0b_ref, 16)

    dest = dest_ref[...]
    upper = (iota((128, 128), 0) <= iota((128, 128), 1)).astype(f32).astype(bf16)
    before = (iota((16, 16), 1) < iota((16, 16), 0)).astype(f32).astype(bf16)
    rank = jnp.zeros((16, 128), f32)
    for k in range(9):
        chosen = (dest == k).astype(f32)
        marks = chosen.astype(bf16)
        inside = dot(marks, upper)
        earlier = jnp.sum(dot(before, marks), axis=1, keepdims=True)
        rank = rank + chosen * (inside - 1.0 + earlier)
    rank_ref[...] = rank.astype(i32)


def prepare(first, taps, dest):
    return pl.pallas_call(
        prep_kernel,
        out_shape=(
            jax.ShapeDtypeStruct((768, 512), bf16),
            jax.ShapeDtypeStruct((9, 256, 256), bf16),
            jax.ShapeDtypeStruct((9, 128, 128), bf16),
            jax.ShapeDtypeStruct((9, 256, 256), bf16),
            jax.ShapeDtypeStruct((9, 512, 512), bf16),
            jax.ShapeDtypeStruct((16, 128), i32),
        ),
        compiler_params=pltpu.CompilerParams(vmem_limit_bytes=24 * 2**20),
        cost_estimate=pl.CostEstimate(
            flops=5_000_000, bytes_accessed=20_000_000, transcendentals=0
        ),
    )(first, taps, dest)


def network_kernel(
    own_ref,
    low_ref,
    high_ref,
    w0a_ref,
    w1a_ref,
    w2_ref,
    w1b_ref,
    w0b_hbm,
    head_ref,
    pool_ref,
    grow_ref,
    pool1_ref,
    grow1_ref,
    rowpool_ref,
    rowgrow_ref,
    pos_ref,
    vel_ref,
    where_ref,
    dest_ref,
    rank_ref,
    out_ref,
    w0b_ref,
    even,
    odd,
    vm,
    v0,
    vp,
    e0_ref,
    p1_ref,
    p2_ref,
    u1_ref,
    ue_ref,
    uo_ref,
    um,
    u0,
    up,
    sem,
):
    fetch = pltpu.make_async_copy(w0b_hbm, w0b_ref, sem)
    fetch.start()

    low = low_ref[...].astype(f32)
    high = high_ref[...].astype(f32)
    own = own_ref[...].astype(f32)
    for parity, ref in ((0, even), (1, odd)):
        ref[0:6, :] = low[6 * parity : 6 * parity + 6]
        ref[6:22, :] = own[16 * parity : 16 * parity + 16]
        ref[22:28, :] = high[6 * parity : 6 * parity + 6]
        ref[28:40, :] = jnp.zeros((12, 2048), f32)

    def spread(value, targets):
        plain = value.astype(bf16)
        rolled = pltpu.roll(value, 2048 - 64, 1).astype(bf16)
        for column in range(COLS):
            if column % 2:
                piece = plain[:, 64 * (column + 1) : 64 * (column + 1) + 256]
            else:
                piece = rolled[:, 64 * column : 64 * column + 256]
            for ref, half in targets:
                begin = column * 64 + half * 32
                ref[begin : begin + 32, :] = piece

    spread(odd[0:32, :], ((vm, 0),))
    spread(even[1:33, :], ((vm, 1), (v0, 0)))
    spread(odd[1:33, :], ((v0, 1), (vp, 0)))
    spread(even[2:34, :], ((vp, 1),))

    p1_ref[0:8, :] = jnp.zeros((8, 256), f32)
    p1_ref[456:464, :] = jnp.zeros((8, 256), f32)

    def fine(block, carry):
        begin = pl.multiple_of(block * 256, 256)
        rows = pl.ds(begin, 256)
        total = dot(vm[rows, :], w0a_ref[0:256, :])
        total = total + dot(v0[rows, :], w0a_ref[256:512, :])
        total = total + dot(vp[rows, :], w0a_ref[512:768, :])
        value = gelu(total).astype(bf16)
        e0_ref[rows, :] = value
        quads = value.astype(f32).reshape(2, 4, 32, 512)
        summed = (quads[:, 0] + quads[:, 1]) + (quads[:, 2] + quads[:, 3])
        pooled = dot(summed.reshape(64, 512).astype(bf16), pool_ref[...])
        p1_ref[pl.ds(pl.multiple_of(8 + block * 64, 8), 64), :] = pooled.astype(bf16).astype(f32)
        return carry

    lax.fori_loop(0, 7, fine, 0)

    def middle(ref, blocks, weight_ref, stride, size, pad):
        shifted = [ref[pad + oy - 1 : pad + oy - 1 + size, :].astype(bf16) for oy in range(3)]
        total = None
        for ox in range(3):
            for oy in range(3):
                piece = shifted[oy][ox * stride : ox * stride + blocks * stride]
                term = dot(piece, weight_ref[ox * 3 + oy])
                total = term if total is None else total + term
        return gelu(total).astype(bf16)

    e1 = middle(p1_ref, 12, w1a_ref, 32, 448, 8)
    part = dot(rowpool_ref[...], e1).astype(bf16)
    p2_ref[0:8, :] = jnp.zeros((8, 128), f32)
    p2_ref[104:112, :] = jnp.zeros((8, 128), f32)
    p2_ref[8:104, :] = dot(part, pool1_ref[...]).astype(bf16).astype(f32)
    e2 = middle(p2_ref, 4, w2_ref, 16, 96, 8)
    grown = dot(dot(rowgrow_ref[...], e2).astype(bf16), grow1_ref[...])
    u1_ref[0:8, :] = jnp.zeros((8, 256), f32)
    u1_ref[264:272, :] = jnp.zeros((8, 256), f32)
    u1_ref[8:264, :] = (e1[64:320].astype(f32) + grown).astype(bf16).astype(f32)
    f1 = middle(u1_ref, 6, w1b_ref, 32, 256, 8)
    grown = dot(f1, grow_ref[...])
    for n in range(10):
        add = grown[((n + 1) // 2) * 32 : ((n + 1) // 2) * 32 + 32]
        begin = (n + 9) * 64
        ue_ref[...] = (e0_ref[begin : begin + 32, :].astype(f32) + add).astype(bf16).astype(f32)
        uo_ref[...] = (e0_ref[begin + 32 : begin + 64, :].astype(f32) + add).astype(bf16).astype(f32)
        at = n * 32
        even_here = ue_ref[5:21, :].astype(bf16)
        odd_here = uo_ref[5:21, :].astype(bf16)
        um[at : at + 16, :] = uo_ref[4:20, :].astype(bf16)
        um[at + 16 : at + 32, :] = even_here
        u0[at : at + 16, :] = even_here
        u0[at + 16 : at + 32, :] = odd_here
        up[at : at + 16, :] = odd_here
        up[at + 16 : at + 32, :] = ue_ref[6:22, :].astype(bf16)

    fetch.wait()
    total = None
    for ox in range(3):
        for oy, ref in enumerate((um, u0, up)):
            term = dot(ref[ox * 32 : ox * 32 + 256, :], w0b_ref[ox * 3 + oy])
            total = term if total is None else total + term
    change = dot(gelu(total).astype(bf16), head_ref[...])

    lane16 = iota((32, 128), 1) // 16
    tables = []
    for comp in range(3):
        table = jnp.zeros((32, 128), f32)
        for x in range(8):
            block = change[x * 32 : x * 32 + 32]
            shift = ((x - comp) * 16) % 128
            moved = pltpu.roll(block, shift, 1) if shift else block
            table = jnp.where(lane16 == x, moved, table)
        tables.append(table)
    cell = where_ref[...]
    y = jnp.bitwise_and(jnp.right_shift(cell, 4), 31)
    row = jnp.bitwise_and(y, 1) * 16 + jnp.right_shift(y, 1)
    lane = jnp.right_shift(cell, 9) * 16 + jnp.bitwise_and(cell, 15)
    kick = [jnp.zeros((16, 128), f32) for _ in range(3)]
    for r in range(32):
        here = row == r
        for comp in range(3):
            source = jnp.broadcast_to(tables[comp][r : r + 1], (16, 128))
            kick[comp] = jnp.where(here, jnp.take_along_axis(source, lane, axis=1), kick[comp])
    payload = []
    speeds = [vel_ref[comp] + kick[comp] for comp in range(3)]
    for comp in range(3):
        payload.append(pos_ref[comp] + DRIFT * speeds[comp])
    payload = payload + speeds

    rank = rank_ref[...]
    key = dest_ref[...] * 4 + jnp.right_shift(rank, 7)
    slot = jnp.bitwise_and(rank, 127)
    line = iota((216, 128), 0)
    line_key = (line // 24) * 4 + jnp.bitwise_and(line, 3)
    slots = iota((128, 128), 0)
    packed = jnp.zeros((216, 128), f32)
    for pair in range(8):
        left, right = [], []
        for c in (2 * pair, 2 * pair + 1):
            rows = jnp.concatenate(
                [jnp.broadcast_to(part[c : c + 1], (4, 128)) for part in payload], axis=0
            )
            full = jnp.concatenate([rows] * 9, axis=0)
            left.append(jnp.where(line_key == key[c : c + 1], full, 0.0).astype(bf16))
            right.append((slots == slot[c : c + 1]).astype(f32).astype(bf16))
        packed = packed + lax.dot_general(
            jnp.concatenate(left, axis=1),
            jnp.concatenate(right, axis=1),
            (((1,), (1,)), ((), ())),
            preferred_element_type=f32,
        )
    out_ref[...] = packed.astype(bf16)


def constants():
    pool = np.zeros((NZ * CH, NZ // 2 * CH), np.float32)
    for z in range(NZ):
        for c in range(CH):
            pool[z * CH + c, z // 2 * CH + c] = 1.0
    pool1 = pool[: 8 * CH, : 4 * CH]
    rowpool = np.zeros((96, 384), np.float32)
    for a in range(6):
        for s in range(12):
            for dx in range(2):
                for dy in range(2):
                    rowpool[a * 16 + s, (2 * a + dx) * 32 + 2 * s + 1 + dy] = 0.25
    rowgrow = np.zeros((256, 64), np.float32)
    for c in range(8):
        for r in range(3, 23):
            rowgrow[c * 32 + r, (c // 2) * 16 + (r - 1) // 2] = 1.0
    made = (pool * 0.125, pool.T, pool1 * 0.5, pool1.T, rowpool, rowgrow)
    return [jnp.asarray(np.ascontiguousarray(value), bf16) for value in made]


def network(own, low, high, weights, head, pos, vel, where, dest, rank):
    w0a, w1a, w2, w1b, w0b = weights
    pool, grow, pool1, grow1, rowpool, rowgrow = constants()
    vmem = pl.BlockSpec(memory_space=pltpu.VMEM)
    specs = [vmem] * 20
    specs[7] = pl.BlockSpec(memory_space=pl.ANY)
    return pl.pallas_call(
        network_kernel,
        out_shape=jax.ShapeDtypeStruct((216, 128), bf16),
        in_specs=specs,
        out_specs=vmem,
        scratch_shapes=[
            pltpu.VMEM((9, 512, 512), bf16),
            pltpu.VMEM((40, 2048), f32),
            pltpu.VMEM((40, 2048), f32),
            pltpu.VMEM((COLS * 64, 256), bf16),
            pltpu.VMEM((COLS * 64, 256), bf16),
            pltpu.VMEM((COLS * 64, 256), bf16),
            pltpu.VMEM((COLS * 64, 512), bf16),
            pltpu.VMEM((464, 256), f32),
            pltpu.VMEM((112, 128), f32),
            pltpu.VMEM((272, 256), f32),
            pltpu.VMEM((32, 512), f32),
            pltpu.VMEM((32, 512), f32),
            pltpu.VMEM((320, 512), bf16),
            pltpu.VMEM((320, 512), bf16),
            pltpu.VMEM((320, 512), bf16),
            pltpu.SemaphoreType.DMA,
        ],
        compiler_params=pltpu.CompilerParams(vmem_limit_bytes=40 * 2**20),
        cost_estimate=pl.CostEstimate(
            flops=3_000_000_000, bytes_accessed=10_000_000, transcendentals=1_000_000
        ),
    )(
        own, low, high, w0a, w1a, w2, w1b, w0b, head,
        pool, grow, pool1, grow1, rowpool, rowgrow,
        pos, vel, where, dest, rank,
    )


def exchange(value, count_x, count_y, rule):
    pairs = []
    for i in range(count_x):
        for j in range(count_y):
            a, b = rule(i, j)
            pairs.append((i * count_y + j, (a % count_x) * count_y + b % count_y))
    return lax.ppermute(value, ("gx", "gy"), pairs)


def body(
    position,
    velocity,
    cell_list,
    slot_weight,
    particle_cell,
    destination,
    lift,
    kernel_0a,
    kernel_1a,
    kernel_2,
    kernel_1b,
    kernel_0b,
    head,
):
    count_x, count_y = lax.axis_size("gx"), lax.axis_size("gy")
    first_core = lax.rem(lax.axis_index("gx"), 2) == 0

    def mate(value):
        return exchange(value, count_x, count_y, lambda i, j: (i ^ 1, j))

    def cross(value):
        return exchange(value, count_x, count_y, lambda i, j: (i + 1 if i % 2 else i - 1, j))

    def along_y(value):
        return exchange(value, count_x, count_y, lambda i, j: (i, j - 1 if i % 2 else j + 1))

    def either(if_first, if_second):
        return jnp.where(first_core, if_first, if_second)

    def cat(parts, axis):
        return jnp.concatenate(parts, axis=axis)

    combined = jnp.sum(
        kernel_0a.astype(f32)[:, :, :, None] * lift[None, None, :, :], axis=2
    )
    first = jnp.tile(combined.transpose(0, 2, 1), (1, 1, 4)).reshape(108, 128)
    taps = jnp.concatenate([kernel_1a, kernel_2, kernel_1b, kernel_0b], axis=0)
    taps = jnp.tile(taps.transpose(0, 2, 1), (1, 1, 4))
    eye = jnp.eye(NZ, dtype=bf16)
    headed = (eye[:, None, None, :] * head.T[None, :, :, None]).reshape(NZ * CH, 3 * NZ)
    headed = jnp.pad(headed, ((0, 0), (0, 128 - 3 * NZ)))
    dest = destination.reshape(16, 128)
    *weights, rank = prepare(first, taps, dest)

    mine = deposit(velocity, cell_list, slot_weight)
    theirs = mate(mine)
    chip = either(cat([mine, theirs], 1), cat([theirs, mine], 1))
    near = cross(either(chip[:, :768], chip[:, 256:]))
    far = mate(near)
    wide = cat([either(near, far), chip, either(far, near)], 1)
    rim = either(cat([wide[10:16], wide[26:32]], 0), cat([wide[0:6], wide[16:22]], 0))
    near = along_y(rim)
    far = mate(either(near[:, 512:], near[:, :2048]))
    near = either(near[:, :2048], near[:, 512:])
    own = either(wide[:, :2048], wide[:, 512:])
    low, high = either(near, far), either(far, near)

    packed = network(
        own,
        low,
        high,
        weights,
        headed,
        position.reshape(3, 16, 128),
        velocity.reshape(3, 16, 128),
        particle_cell.reshape(16, 128),
        dest,
        rank,
    )

    behind, level, ahead = packed[0:72], packed[72:144], packed[144:216]
    from_mate = mate(either(ahead, behind))
    from_cross = cross(either(behind, ahead))
    behind = either(from_mate, from_cross)
    ahead = either(from_cross, from_mate)
    groups = (behind, level, ahead)
    down = cat([group[0:24] for group in groups], 0)
    upward = cat([group[48:72] for group in groups], 0)
    passed = mate(either(down, upward))
    near = along_y(cat([either(upward, down), passed], 0))
    far = mate(near[72:])
    near = near[:72]
    upward, down = either(near, far), either(far, near)
    blocks = []
    for a in range(3):
        blocks.append(down[24 * a : 24 * a + 24])
        blocks.append(groups[a][24:48])
        blocks.append(upward[24 * a : 24 * a + 24])
    inbox = jnp.stack(blocks, axis=0).reshape(9, 6, CAP)
    return inbox.astype(f32).transpose(1, 0, 2).reshape(6, 9 * CAP)


def solution(mesh):
    in_specs = (
        P(None, ("gx", "gy")),
        P(None, ("gx", "gy")),
        P(None, "gx", "gy", None),
        P(None, "gx", "gy", None),
        P(("gx", "gy")),
        P(("gx", "gy"), None),
        P(),
        P(),
        P(),
        P(),
        P(),
        P(),
        P(),
    )
    out_specs = P(None, ("gx", "gy"))
    return jax.shard_map(body, mesh=mesh, in_specs=in_specs, out_specs=out_specs, check_vma=False)
```

```python
import jax
import jax.numpy as jnp
import numpy as np
from jax import lax
from jax.experimental import pallas as pl
from jax.experimental.pallas import tpu as pltpu
from jax.sharding import PartitionSpec as P

f32 = jnp.float32
bf16 = jnp.bfloat16
i32 = jnp.int32

CAP = 512
DRIFT = 0.25
CH = 32
NZ = 16
COLS = 28


def iota(shape, dim):
    return lax.broadcasted_iota(i32, shape, dim)


def dot(a, b):
    return jnp.dot(a, b, preferred_element_type=f32)


def gelu(x):
    inner = x * (0.7978845608028654 + 0.035677408136300125 * (x * x))
    return (0.5 * x) * (1.0 + jnp.tanh(inner))


def pick_lanes(table, lane):
    numbers = lax.GatherDimensionNumbers(
        offset_dims=(),
        collapsed_slice_dims=(1,),
        start_index_map=(1,),
        operand_batching_dims=(0,),
        start_indices_batching_dims=(0,),
    )
    return lax.gather(
        table,
        lane[..., None],
        numbers,
        (1, 1),
        mode=lax.GatherScatterMode.PROMISE_IN_BOUNDS,
    )


def fetch_all(pairs, sems):
    copies = [
        pltpu.make_async_copy(source, target, sems.at[index])
        for index, (source, target) in enumerate(pairs)
    ]
    for copy in copies:
        copy.start()
    return copies


def deposit_kernel(
    vel_hbm, cells_hbm, weight_hbm, out_ref, stage, vel_ref, cells_ref, weight_ref, sems
):
    fetch_vel, fetch_cells, fetch_weight = fetch_all(
        ((vel_hbm, vel_ref), (cells_hbm, cells_ref), (weight_hbm, weight_ref)), sems
    )

    def dense(ref, s):
        return jnp.concatenate(
            [jnp.concatenate([ref[s, 2 * a + b] for a in range(4)], axis=1) for b in range(2)],
            axis=0,
        )

    fetch_vel.wait()
    fetch_cells.wait()
    entries, picked = [], []
    for s in range(4):
        entry = dense(cells_ref, s)
        lane = jnp.bitwise_and(entry, 127)
        row = jnp.right_shift(entry, 7)
        found = [jnp.zeros((32, 128), f32) for _ in range(3)]
        for r in range(16):
            here = row == r
            for q in range(3):
                table = jnp.broadcast_to(vel_ref[q : q + 1, r * 128 : (r + 1) * 128], (32, 128))
                found[q] = jnp.where(here, pick_lanes(table, lane), found[q])
        entries.append(entry)
        picked.append(found)
    fetch_weight.wait()
    totals = [jnp.zeros((32, 128), f32) for _ in range(4)]
    for s in range(4):
        weight = dense(weight_ref, s)
        totals[0] = totals[0] + jnp.where(entries[s] < 2048, weight, 0.0)
        for q in range(3):
            totals[q + 1] = totals[q + 1] + weight * picked[s][q]
    stage[...] = jnp.concatenate(
        [totals[q][b * 16 : b * 16 + 16] for b in range(2) for q in range(4)], axis=0
    ).T
    for t in range(4):
        for parity in range(2):
            lanes = slice((t % 2) * 128, (t % 2) * 128 + 128)
            out_ref[t // 2, parity * 16 : parity * 16 + 16, lanes] = stage[
                pl.ds(t * 32 + parity, 16, stride=2), :
            ].astype(bf16)


def deposit(velocity, cells, weight):
    return pl.pallas_call(
        deposit_kernel,
        out_shape=pltpu.VMEM((2, 32, 256), bf16),
        in_specs=[pl.BlockSpec(memory_space=pltpu.HBM)] * 3,
        out_specs=pl.BlockSpec(memory_space=pltpu.VMEM),
        scratch_shapes=[
            pltpu.VMEM((128, 128), f32),
            pltpu.VMEM((3, 2048), f32),
            pltpu.VMEM((4, 8, 16, 32), i32),
            pltpu.VMEM((4, 8, 16, 32), f32),
            pltpu.SemaphoreType.DMA((3,)),
        ],
        cost_estimate=pl.CostEstimate(flops=2_000_000, bytes_accessed=1_000_000, transcendentals=0),
    )(velocity, jnp.swapaxes(cells, 2, 3), jnp.swapaxes(weight, 2, 3))


def contract_last(a, b):
    return lax.dot_general(a, b, (((1,), (1,)), ((), ())), preferred_element_type=f32)


def first_kernel(lift_hbm, kernel_hbm, after_ref, w0a_ref, lift_ref, kernel_ref, sems):
    fetch_lift, fetch = fetch_all(((lift_hbm, lift_ref), (kernel_hbm, kernel_ref)), sems)
    fetch_lift.wait()
    rest = lift_ref[...]
    terms = []
    for _ in range(3):
        term = rest.astype(bf16).astype(f32)
        terms.append(term)
        rest = rest - term
    terms = jnp.concatenate(terms + [jnp.zeros((4, 32), f32)], axis=0).astype(bf16)
    row = iota((16, 128), 0)
    masks = []
    for t in range(4):
        diff = jnp.bitwise_and(row - (4 * t + iota((16, 128), 1) // 32), 15)
        masks.append((diff == 15, diff == 0, diff == 1))
    fetch.wait()
    for ox in range(3):
        for oy in range(3):
            at = 9 * ox + 3 * oy
            repeated = [kernel_ref[at + oz] for oz in range(3) for _ in range(4)]
            parts = contract_last(terms, jnp.concatenate(repeated, axis=0))
            both = parts[0:4] + parts[4:8] + parts[8:12]
            for q in range(4):
                low, mid, high = (
                    jnp.broadcast_to(both[q : q + 1, oz * 128 : oz * 128 + 128], (16, 128))
                    for oz in range(3)
                )
                for t in range(4):
                    below, same, above = masks[t]
                    piece = jnp.where(
                        same, mid, jnp.where(below, low, jnp.where(above, high, 0.0))
                    )
                    begin = oy * 256 + ox * 64 + q * 16
                    w0a_ref[begin : begin + 16, t * 128 : (t + 1) * 128] = piece.astype(bf16)
    for oy in range(3):
        w0a_ref[oy * 256 + 192 : oy * 256 + 256, :] = jnp.zeros((64, 512), bf16)


def bands(kernel_ref, out_ref, depth):
    group = iota((32, 128), 1) // 32
    zero = jnp.zeros((32, 128), f32)
    tiles = depth // 4

    def one(tap, carry):
        row = jnp.concatenate(
            [kernel_ref[3 * tap + oz].astype(f32) for oz in range(3)] + [zero[:, 0:32]], axis=1
        )
        turned = jnp.concatenate([row] * 4, axis=0).T
        low, mid, high = (turned[oz * 32 : oz * 32 + 32] for oz in range(3))

        def pick(*wanted):
            value = zero
            for index, piece in wanted:
                value = jnp.where(group == index, piece, value)
            return value

        patterns = (
            {0: pick((0, mid), (1, low)), -1: pick((3, high))},
            {0: pick((0, high), (1, mid), (2, low))},
            {0: pick((1, high), (2, mid), (3, low))},
            {0: pick((2, high), (3, mid)), 1: pick((0, low))},
        )
        for z in range(depth):
            content = {}
            for step, piece in patterns[z % 4].items():
                tile = (z // 4 + step) % tiles
                content[tile] = content[tile] + piece if tile in content else piece
            for tile in range(tiles):
                out_ref[tap, z * 32 : (z + 1) * 32, tile * 128 : (tile + 1) * 128] = (
                    content.get(tile, zero).astype(bf16)
                )
        return carry

    lax.fori_loop(0, 9, one, 0, unroll=3)


def middle_kernel(k1a_hbm, k2_hbm, after_ref, w1a_ref, w2_ref, k1a_ref, k2_ref, sems):
    fetches = fetch_all(((k1a_hbm, k1a_ref), (k2_hbm, k2_ref)), sems)
    for fetch, ref, out_ref, depth in zip(fetches, (k1a_ref, k2_ref), (w1a_ref, w2_ref), (8, 4)):
        fetch.wait()
        bands(ref, out_ref, depth)


def last_kernel(
    head_hbm, dest_hbm, k1b_hbm, k0b_hbm, after_ref, w1b_ref, w0b_ref, headed_ref, rank_ref,
    head_ref, dest_ref, k1b_ref, k0b_ref, sems,
):
    fetches = fetch_all(
        (
            (head_hbm, head_ref), (dest_hbm, dest_ref), (k1b_hbm, k1b_ref), (k0b_hbm, k0b_ref)
        ),
        sems,
    )
    for fetch in fetches:
        fetch.wait()
    bands(k1b_ref, w1b_ref, 8)
    bands(k0b_ref, w0b_ref, 16)

    row16 = iota((16, 128), 0)
    names = head_ref[...].astype(f32)
    names = jnp.concatenate([names] * 4, axis=1)
    for t in range(4):
        same = row16 == 4 * t + iota((16, 128), 1) // 32
        rows = [
            jnp.where(same, jnp.broadcast_to(names[k : k + 1], (16, 128)), 0.0) for k in range(3)
        ]
        rows.append(jnp.zeros((80, 128), f32))
        headed_ref[t * 128 : t * 128 + 128, :] = jnp.concatenate(rows, axis=0).T.astype(bf16)

    dest = dest_ref[...]
    upper = (iota((128, 128), 0) <= iota((128, 128), 1)).astype(f32).astype(bf16)
    before = (iota((16, 16), 1) < iota((16, 16), 0)).astype(f32).astype(bf16)
    rank = jnp.zeros((16, 128), f32)
    for k in range(9):
        chosen = (dest == k).astype(f32)
        marks = chosen.astype(bf16)
        inside = dot(marks, upper)
        earlier = jnp.sum(dot(before, marks), axis=1, keepdims=True)
        rank = rank + chosen * (inside - 1.0 + earlier)
    rank_ref[...] = rank.astype(i32)


def first_weights(kernel, lift, after):
    hbm = pl.BlockSpec(memory_space=pltpu.HBM)
    any_ = pl.BlockSpec(memory_space=pl.ANY)
    vmem = pl.BlockSpec(memory_space=pltpu.VMEM)
    return pl.pallas_call(
        first_kernel,
        out_shape=jax.ShapeDtypeStruct((768, 512), bf16),
        in_specs=[hbm, hbm, any_],
        out_specs=vmem,
        scratch_shapes=[
            pltpu.VMEM((4, 32), f32),
            pltpu.VMEM((27, 32, 32), bf16),
            pltpu.SemaphoreType.DMA((2,)),
        ],
        compiler_params=pltpu.CompilerParams(vmem_limit_bytes=8 * 2**20),
        cost_estimate=pl.CostEstimate(flops=500_000, bytes_accessed=2_000_000, transcendentals=0),
    )(lift, kernel, after)


def middle_weights(kernels, after):
    hbm = pl.BlockSpec(memory_space=pltpu.HBM)
    any_ = pl.BlockSpec(memory_space=pl.ANY)
    vmem = pl.BlockSpec(memory_space=pltpu.VMEM)
    return pl.pallas_call(
        middle_kernel,
        out_shape=(
            jax.ShapeDtypeStruct((9, 256, 256), bf16),
            jax.ShapeDtypeStruct((9, 128, 128), bf16),
        ),
        in_specs=[hbm, hbm, any_],
        out_specs=(vmem,) * 2,
        scratch_shapes=[pltpu.VMEM((27, 32, 32), bf16)] * 2 + [pltpu.SemaphoreType.DMA((2,))],
        compiler_params=pltpu.CompilerParams(vmem_limit_bytes=12 * 2**20),
        cost_estimate=pl.CostEstimate(
            flops=5_000_000, bytes_accessed=5_000_000, transcendentals=0
        ),
    )(*kernels, after)


def last_weights(head, dest, kernels, after):
    hbm = pl.BlockSpec(memory_space=pltpu.HBM)
    any_ = pl.BlockSpec(memory_space=pl.ANY)
    vmem = pl.BlockSpec(memory_space=pltpu.VMEM)
    return pl.pallas_call(
        last_kernel,
        out_shape=(
            jax.ShapeDtypeStruct((9, 256, 256), bf16),
            jax.ShapeDtypeStruct((9, 512, 512), bf16),
            jax.ShapeDtypeStruct((512, 128), bf16),
            jax.ShapeDtypeStruct((16, 128), i32),
        ),
        in_specs=[hbm] * 4 + [any_],
        out_specs=(vmem,) * 4,
        scratch_shapes=[
            pltpu.VMEM((3, 32), bf16),
            pltpu.VMEM((16, 128), i32),
            pltpu.VMEM((27, 32, 32), bf16),
            pltpu.VMEM((27, 32, 32), bf16),
            pltpu.SemaphoreType.DMA((4,)),
        ],
        compiler_params=pltpu.CompilerParams(vmem_limit_bytes=16 * 2**20),
        cost_estimate=pl.CostEstimate(
            flops=5_000_000, bytes_accessed=5_000_000, transcendentals=0
        ),
    )(head, dest, *kernels, after)


def lanes_of(ref):
    return jnp.concatenate([ref[chunk].astype(f32) for chunk in range(8)], axis=1)


def spread(value, taps_ref, targets):
    plain = value.astype(bf16)
    rolled = pltpu.roll(value, 2048 - 64, 1).astype(bf16)
    for column in range(COLS):
        if column % 2:
            piece = plain[:, 64 * (column + 1) : 64 * (column + 1) + 256]
        else:
            piece = rolled[:, 64 * column : 64 * column + 256]
        for oy, half in targets:
            begin = column * 32 + half * 16
            taps_ref[begin : begin + 16, oy * 256 : oy * 256 + 256] = piece


def first_conv(taps_ref, weight_ref, sums_ref, keep):
    for block in range(COLS // 4):
        value = gelu(dot(taps_ref[block * 128 : block * 128 + 128, :], weight_ref[...])).astype(bf16)
        keep(block, value)
        quads = value.astype(f32).reshape(2, 4, 16, 512)
        summed = (quads[:, 0] + quads[:, 1]) + (quads[:, 2] + quads[:, 3])
        sums_ref[block * 32 : block * 32 + 32, :] = summed.reshape(32, 512).astype(bf16)


def own_kernel(own_ref, w0a_ref, pool_ref, e0_ref, p1_ref, taps, sums):
    own = lanes_of(own_ref)
    even, odd = own[0:16], own[16:32]
    spread(pltpu.roll(odd, 1, 0), taps, ((0, 0),))
    spread(even, taps, ((0, 1), (1, 0)))
    spread(odd, taps, ((1, 1), (2, 0)))
    spread(pltpu.roll(even, 15, 0), taps, ((2, 1),))

    def keep(block, value):
        for column in range(4):
            n = block * 4 + column - 9
            if 0 <= n < 10:
                e0_ref[n * 32 : n * 32 + 32, :] = value[column * 32 : column * 32 + 32]

    first_conv(taps, w0a_ref, sums, keep)
    p1_ref[...] = dot(sums[...], pool_ref[...]).astype(bf16)


def own_part(own, w0a, pool):
    return pl.pallas_call(
        own_kernel,
        out_shape=(
            jax.ShapeDtypeStruct((320, 512), bf16),
            jax.ShapeDtypeStruct((224, 256), bf16),
        ),
        scratch_shapes=[pltpu.VMEM((COLS * 32, 768), bf16), pltpu.VMEM((224, 512), bf16)],
        compiler_params=pltpu.CompilerParams(vmem_limit_bytes=16 * 2**20),
        cost_estimate=pl.CostEstimate(
            flops=2_000_000_000, bytes_accessed=2_000_000, transcendentals=500_000
        ),
    )(own, w0a, pool)


def network_kernel(
    own_ref,
    low_ref,
    high_ref,
    own_e0_ref,
    own_p1_ref,
    w0a_ref,
    w1a_ref,
    w2_ref,
    w1b_ref,
    w0b_hbm,
    head_ref,
    pool_ref,
    grow_ref,
    pool1_ref,
    grow1_ref,
    rowpool_ref,
    rowgrow_ref,
    pos_ref,
    vel_ref,
    where_ref,
    dest_ref,
    rank_ref,
    out_ref,
    w0b_ref,
    even,
    odd,
    taps,
    sums,
    e0_ref,
    p1_ref,
    p2_ref,
    u1_ref,
    ue_ref,
    uo_ref,
    um,
    u0,
    up,
    sem,
):
    fetch = pltpu.make_async_copy(w0b_hbm, w0b_ref, sem)
    fetch.start()

    low = lanes_of(low_ref)
    high = lanes_of(high_ref)
    own = lanes_of(own_ref)
    for parity, ref in ((0, even), (1, odd)):
        ref[0:2, :] = jnp.zeros((2, 2048), f32)
        ref[2:8, :] = low[6 * parity : 6 * parity + 6]
        ref[8:24, :] = own[16 * parity : 16 * parity + 16]
        ref[24:30, :] = high[6 * parity : 6 * parity + 6]
        ref[30:32, :] = jnp.zeros((2, 2048), f32)

    def outer(ref, first):
        return jnp.concatenate([ref[first : first + 8, :], ref[first + 22 : first + 30, :]], axis=0)

    spread(outer(odd, 0), taps, ((0, 0),))
    spread(outer(even, 1), taps, ((0, 1), (1, 0)))
    spread(outer(odd, 1), taps, ((1, 1), (2, 0)))
    spread(outer(even, 2), taps, ((2, 1),))

    for n in range(10):
        for parity in range(2):
            at = n * 64 + parity * 32
            begin = n * 32 + parity * 16
            e0_ref[at + 8 : at + 24, :] = own_e0_ref[begin : begin + 16, :].astype(f32)

    def keep(block, value):
        for column in range(4):
            n = block * 4 + column - 9
            if 0 <= n < 10:
                for parity in range(2):
                    at = n * 64 + parity * 32
                    begin = column * 32 + parity * 16
                    rows = value[begin : begin + 16].astype(f32)
                    e0_ref[at + 1 : at + 9, :] = rows[0:8]
                    e0_ref[at + 23 : at + 31, :] = rows[8:16]

    first_conv(taps, w0a_ref, sums, keep)
    pooled = dot(sums[...], pool_ref[...]).astype(bf16).astype(f32)
    own_pooled = own_p1_ref[...].astype(f32)
    p1_ref[...] = jnp.zeros((464, 256), f32)
    for column in range(14):
        at = 8 + column * 32
        p1_ref[at + 8 : at + 24, :] = own_pooled[column * 16 : column * 16 + 16]
        p1_ref[at + 1 : at + 9, :] = pooled[column * 16 : column * 16 + 8]
        p1_ref[at + 23 : at + 31, :] = pooled[column * 16 + 8 : column * 16 + 16]

    def middle(ref, blocks, weight_ref, stride, size, pad):
        shifted = [ref[pad + oy - 1 : pad + oy - 1 + size, :].astype(bf16) for oy in range(3)]
        total = None
        for ox in range(3):
            for oy in range(3):
                piece = shifted[oy][ox * stride : ox * stride + blocks * stride]
                term = dot(piece, weight_ref[ox * 3 + oy])
                total = term if total is None else total + term
        return gelu(total).astype(bf16)

    e1 = middle(p1_ref, 12, w1a_ref, 32, 448, 8)
    part = dot(rowpool_ref[...], e1).astype(bf16)
    p2_ref[0:8, :] = jnp.zeros((8, 128), f32)
    p2_ref[104:112, :] = jnp.zeros((8, 128), f32)
    p2_ref[8:104, :] = dot(part, pool1_ref[...]).astype(bf16).astype(f32)
    e2 = middle(p2_ref, 4, w2_ref, 16, 96, 8)
    grown = dot(dot(rowgrow_ref[...], e2).astype(bf16), grow1_ref[...])
    u1_ref[0:8, :] = jnp.zeros((8, 256), f32)
    u1_ref[264:272, :] = jnp.zeros((8, 256), f32)
    u1_ref[8:264, :] = (e1[64:320].astype(f32) + grown).astype(bf16).astype(f32)
    f1 = middle(u1_ref, 6, w1b_ref, 32, 256, 8)
    grown = dot(f1, grow_ref[...])
    for n in range(10):
        add = grown[((n + 1) // 2) * 32 : ((n + 1) // 2) * 32 + 32]
        begin = n * 64
        ue_ref[...] = (e0_ref[begin : begin + 32, :] + add).astype(bf16).astype(f32)
        uo_ref[...] = (e0_ref[begin + 32 : begin + 64, :] + add).astype(bf16).astype(f32)
        at = n * 32
        even_here = ue_ref[8:24, :].astype(bf16)
        odd_here = uo_ref[8:24, :].astype(bf16)
        um[at : at + 16, :] = uo_ref[7:23, :].astype(bf16)
        um[at + 16 : at + 32, :] = even_here
        u0[at : at + 16, :] = even_here
        u0[at + 16 : at + 32, :] = odd_here
        up[at : at + 16, :] = odd_here
        up[at + 16 : at + 32, :] = ue_ref[9:25, :].astype(bf16)

    fetch.wait()
    total = None
    for ox in range(3):
        for oy, ref in enumerate((um, u0, up)):
            term = dot(ref[ox * 32 : ox * 32 + 256, :], w0b_ref[ox * 3 + oy])
            total = term if total is None else total + term
    change = dot(gelu(total).astype(bf16), head_ref[...])

    lane16 = iota((32, 128), 1) // 16
    tables = []
    for comp in range(3):
        table = jnp.zeros((32, 128), f32)
        for x in range(8):
            block = change[x * 32 : x * 32 + 32]
            shift = ((x - comp) * 16) % 128
            moved = pltpu.roll(block, shift, 1) if shift else block
            table = jnp.where(lane16 == x, moved, table)
        tables.append(table)
    cell = where_ref[...]
    y = jnp.bitwise_and(jnp.right_shift(cell, 4), 31)
    row = jnp.bitwise_and(y, 1) * 16 + jnp.right_shift(y, 1)
    lane = jnp.right_shift(cell, 9) * 16 + jnp.bitwise_and(cell, 15)
    kick = [jnp.zeros((16, 128), f32) for _ in range(3)]
    for r in range(32):
        here = row == r
        for comp in range(3):
            source = jnp.broadcast_to(tables[comp][r : r + 1], (16, 128))
            kick[comp] = jnp.where(here, pick_lanes(source, lane), kick[comp])
    payload = []
    speeds = [vel_ref[comp] + kick[comp] for comp in range(3)]
    for comp in range(3):
        payload.append(pos_ref[comp] + DRIFT * speeds[comp])
    payload = payload + speeds

    rank = rank_ref[...]
    key = dest_ref[...] * 4 + jnp.right_shift(rank, 7)
    slot = jnp.bitwise_and(rank, 127)
    line = iota((216, 128), 0)
    line_key = (line // 24) * 4 + jnp.bitwise_and(line, 3)
    slots = iota((128, 128), 0)
    packed = jnp.zeros((216, 128), f32)
    for pair in range(8):
        left, right = [], []
        for c in (2 * pair, 2 * pair + 1):
            rows = jnp.concatenate(
                [jnp.broadcast_to(part[c : c + 1], (4, 128)) for part in payload], axis=0
            )
            full = jnp.concatenate([rows] * 9, axis=0)
            left.append(jnp.where(line_key == key[c : c + 1], full, 0.0).astype(bf16))
            right.append((slots == slot[c : c + 1]).astype(f32).astype(bf16))
        packed = packed + contract_last(
            jnp.concatenate(left, axis=1), jnp.concatenate(right, axis=1)
        )
    out_ref[...] = packed.astype(bf16)


def constants():
    pool = np.zeros((NZ * CH, NZ // 2 * CH), np.float32)
    for z in range(NZ):
        for c in range(CH):
            pool[z * CH + c, z // 2 * CH + c] = 1.0
    pool1 = pool[: 8 * CH, : 4 * CH]
    rowpool = np.zeros((96, 384), np.float32)
    for a in range(6):
        for s in range(12):
            for dx in range(2):
                for dy in range(2):
                    rowpool[a * 16 + s, (2 * a + dx) * 32 + 2 * s + 4 + dy] = 0.25
    rowgrow = np.zeros((256, 64), np.float32)
    for c in range(8):
        for r in range(6, 26):
            rowgrow[c * 32 + r, (c // 2) * 16 + (r - 4) // 2] = 1.0
    made = (pool * 0.125, pool.T, pool1 * 0.5, pool1.T, rowpool, rowgrow)
    return [jnp.asarray(np.ascontiguousarray(value), bf16) for value in made]


def network(own, low, high, fine, weights, head, fixed, pos, vel, where, dest, rank):
    vmem = pl.BlockSpec(memory_space=pltpu.VMEM)
    specs = [vmem] * 22
    specs[9] = pl.BlockSpec(memory_space=pl.ANY)
    return pl.pallas_call(
        network_kernel,
        out_shape=jax.ShapeDtypeStruct((216, 128), bf16),
        in_specs=specs,
        out_specs=vmem,
        scratch_shapes=[
            pltpu.VMEM((9, 512, 512), bf16),
            pltpu.VMEM((32, 2048), f32),
            pltpu.VMEM((32, 2048), f32),
            pltpu.VMEM((COLS * 32, 768), bf16),
            pltpu.VMEM((224, 512), bf16),
            pltpu.VMEM((640, 512), f32),
            pltpu.VMEM((464, 256), f32),
            pltpu.VMEM((112, 128), f32),
            pltpu.VMEM((272, 256), f32),
            pltpu.VMEM((32, 512), f32),
            pltpu.VMEM((32, 512), f32),
            pltpu.VMEM((320, 512), bf16),
            pltpu.VMEM((320, 512), bf16),
            pltpu.VMEM((320, 512), bf16),
            pltpu.SemaphoreType.DMA,
        ],
        compiler_params=pltpu.CompilerParams(vmem_limit_bytes=36 * 2**20),
        cost_estimate=pl.CostEstimate(
            flops=3_000_000_000, bytes_accessed=10_000_000, transcendentals=1_000_000
        ),
    )(own, low, high, *fine, *weights, head, *fixed, pos, vel, where, dest, rank)


def exchange(value, count_x, count_y, rule):
    pairs = []
    for i in range(count_x):
        for j in range(count_y):
            a, b = rule(i, j)
            pairs.append((i * count_y + j, (a % count_x) * count_y + b % count_y))
    return lax.ppermute(value, ("gx", "gy"), pairs)


def body(
    position,
    velocity,
    cell_list,
    slot_weight,
    particle_cell,
    destination,
    lift,
    kernel_0a,
    kernel_1a,
    kernel_2,
    kernel_1b,
    kernel_0b,
    head,
):
    count_x, count_y = lax.axis_size("gx"), lax.axis_size("gy")
    first_core = lax.rem(lax.axis_index("gx"), 2) == 0

    def mate(value):
        return exchange(value, count_x, count_y, lambda i, j: (i ^ 1, j))

    def cross(value):
        return exchange(value, count_x, count_y, lambda i, j: (i + 1 if i % 2 else i - 1, j))

    def along_y(value):
        return exchange(value, count_x, count_y, lambda i, j: (i, j - 1 if i % 2 else j + 1))

    def either(if_first, if_second):
        return jnp.where(first_core, if_first, if_second)

    def cat(parts, axis):
        return jnp.concatenate(parts, axis=axis)

    def barrier(*values):
        return lax.optimization_barrier(values)

    fixed = constants()
    dest = destination.reshape(16, 128)

    mine = deposit(velocity, cell_list, slot_weight)
    theirs = mate(mine)
    near = cross(cat([mine, either(theirs[0:1], theirs[1:2])], 0))
    chip = cat([either(mine, theirs), either(theirs, mine)], 0)

    w0a = first_weights(kernel_0a, lift.T, mine)
    w1a, w2 = middle_weights((kernel_1a, kernel_2), theirs)
    near, w0a, w1a, w2 = barrier(near, w0a, w1a, w2)
    far = mate(near)
    left, right = either(near, far), either(far, near)
    wide = cat([left[2:3], left[0:2], chip, right], 0)
    near = along_y(
        either(
            cat([wide[:, 10:16], wide[:, 26:32]], 1), cat([wide[:, 0:6], wide[:, 16:22]], 1)
        )
    )
    own = either(wide[0:8], wide[2:10])
    fine = own_part(own, w0a, fixed[0])
    w1b, w0b, headed, rank = last_weights(head, dest, (kernel_1b, kernel_0b), own)
    weights = (w0a, w1a, w2, w1b, w0b)
    near, fine, weights, headed, rank = barrier(near, fine, weights, headed, rank)
    far = mate(either(near[2:10], near[0:8]))
    near = either(near[0:8], near[2:10])
    low, high = either(near, far), either(far, near)

    packed = network(
        own,
        low,
        high,
        fine,
        weights,
        headed,
        fixed,
        position.reshape(3, 16, 128),
        velocity.reshape(3, 16, 128),
        particle_cell.reshape(16, 128),
        dest,
        rank,
    )

    behind, level, ahead = packed[0:72], packed[72:144], packed[144:216]
    from_mate = mate(either(ahead, behind))
    from_cross = cross(either(behind, ahead))
    behind = either(from_mate, from_cross)
    ahead = either(from_cross, from_mate)
    groups = (behind, level, ahead)
    down = cat([group[0:24] for group in groups], 0)
    upward = cat([group[48:72] for group in groups], 0)
    passed = mate(either(down, upward))
    near = along_y(cat([either(upward, down), passed], 0))
    far = mate(near[72:])
    near = near[:72]
    upward, down = either(near, far), either(far, near)
    blocks = []
    for a in range(3):
        blocks.append(down[24 * a : 24 * a + 24])
        blocks.append(groups[a][24:48])
        blocks.append(upward[24 * a : 24 * a + 24])
    inbox = jnp.stack(blocks, axis=0).reshape(9, 6, CAP)
    return inbox.astype(f32).transpose(1, 0, 2).reshape(6, 9 * CAP)


def solution(mesh):
    in_specs = (
        P(None, ("gx", "gy")),
        P(None, ("gx", "gy")),
        P(None, "gx", "gy", None),
        P(None, "gx", "gy", None),
        P(("gx", "gy")),
        P(("gx", "gy"), None),
        P(),
        P(),
        P(),
        P(),
        P(),
        P(),
        P(),
    )
    out_specs = P(None, ("gx", "gy"))
    return jax.shard_map(body, mesh=mesh, in_specs=in_specs, out_specs=out_specs, check_vma=False)
```

```python
import jax
import jax.numpy as jnp
import numpy as np
from jax import lax
from jax.experimental import pallas as pl
from jax.experimental.pallas import tpu as pltpu
from jax.sharding import PartitionSpec as P

f32 = jnp.float32
bf16 = jnp.bfloat16
i32 = jnp.int32

CAP = 512
DRIFT = 0.25
CH = 32
NZ = 16
COLS = 28


def iota(shape, dim):
    return lax.broadcasted_iota(i32, shape, dim)


def dot(a, b):
    return jnp.dot(a, b, preferred_element_type=f32)


def gelu(x):
    inner = x * (0.7978845608028654 + 0.035677408136300125 * (x * x))
    return (0.5 * x) * (1.0 + jnp.tanh(inner))


def pick_lanes(table, lane):
    numbers = lax.GatherDimensionNumbers(
        offset_dims=(),
        collapsed_slice_dims=(1,),
        start_index_map=(1,),
        operand_batching_dims=(0,),
        start_indices_batching_dims=(0,),
    )
    return lax.gather(
        table,
        lane[..., None],
        numbers,
        (1, 1),
        mode=lax.GatherScatterMode.PROMISE_IN_BOUNDS,
    )


def fetch_all(pairs, sems):
    copies = [
        pltpu.make_async_copy(source, target, sems.at[index])
        for index, (source, target) in enumerate(pairs)
    ]
    for copy in copies:
        copy.start()
    return copies


def deposit_kernel(*refs):
    vel_hbm, cells_hbm, weight_hbm = refs[:3]
    raw_in, out_ref, raw_out = refs[3:11], refs[11], refs[12:20]
    stage, vel_ref, cells_ref, weight_ref, sems, raw_sems = refs[20:]
    fetch_vel, fetch_cells, fetch_weight = fetch_all(
        ((vel_hbm, vel_ref), (cells_hbm, cells_ref), (weight_hbm, weight_ref)), sems
    )
    raw_fetches = fetch_all(zip(raw_in, raw_out), raw_sems)

    def dense(ref, s):
        return jnp.concatenate(
            [jnp.concatenate([ref[s, 2 * a + b] for a in range(4)], axis=1) for b in range(2)],
            axis=0,
        )

    fetch_vel.wait()
    fetch_cells.wait()
    entries, picked = [], []
    for s in range(4):
        entry = dense(cells_ref, s)
        lane = jnp.bitwise_and(entry, 127)
        row = jnp.right_shift(entry, 7)
        found = [jnp.zeros((32, 128), f32) for _ in range(3)]
        for r in range(16):
            here = row == r
            for q in range(3):
                table = jnp.broadcast_to(vel_ref[q : q + 1, r * 128 : (r + 1) * 128], (32, 128))
                found[q] = jnp.where(here, pick_lanes(table, lane), found[q])
        entries.append(entry)
        picked.append(found)
    fetch_weight.wait()
    totals = [jnp.zeros((32, 128), f32) for _ in range(4)]
    for s in range(4):
        weight = dense(weight_ref, s)
        totals[0] = totals[0] + jnp.where(entries[s] < 2048, weight, 0.0)
        for q in range(3):
            totals[q + 1] = totals[q + 1] + weight * picked[s][q]
    stage[...] = jnp.concatenate(
        [totals[q][b * 16 : b * 16 + 16] for b in range(2) for q in range(4)], axis=0
    ).T
    for t in range(4):
        for parity in range(2):
            lanes = slice((t % 2) * 128, (t % 2) * 128 + 128)
            out_ref[t // 2, parity * 16 : parity * 16 + 16, lanes] = stage[
                pl.ds(t * 32 + parity, 16, stride=2), :
            ].astype(bf16)
    for fetch in raw_fetches:
        fetch.wait()


def deposit(velocity, cells, weight, raw):
    return pl.pallas_call(
        deposit_kernel,
        out_shape=(
            pltpu.VMEM((2, 32, 256), bf16),
            *(pltpu.VMEM(value.shape, value.dtype) for value in raw),
        ),
        in_specs=[pl.BlockSpec(memory_space=pltpu.HBM)] * 11,
        out_specs=[pl.BlockSpec(memory_space=pltpu.VMEM)] * 9,
        scratch_shapes=[
            pltpu.VMEM((128, 128), f32),
            pltpu.VMEM((3, 2048), f32),
            pltpu.VMEM((4, 8, 16, 32), i32),
            pltpu.VMEM((4, 8, 16, 32), f32),
            pltpu.SemaphoreType.DMA((3,)),
            pltpu.SemaphoreType.DMA((8,)),
        ],
        cost_estimate=pl.CostEstimate(flops=2_000_000, bytes_accessed=1_000_000, transcendentals=0),
    )(velocity, jnp.swapaxes(cells, 2, 3), jnp.swapaxes(weight, 2, 3), *raw)


def contract_last(a, b):
    return lax.dot_general(a, b, (((1,), (1,)), ((), ())), preferred_element_type=f32)


def first_kernel(lift_ref, kernel_ref, w0a_ref):
    rest = lift_ref[...]
    terms = []
    for _ in range(3):
        term = rest.astype(bf16).astype(f32)
        terms.append(term)
        rest = rest - term
    terms = jnp.concatenate(terms + [jnp.zeros((4, 32), f32)], axis=0).astype(bf16)
    row = iota((16, 128), 0)
    masks = []
    for t in range(4):
        diff = jnp.bitwise_and(row - (4 * t + iota((16, 128), 1) // 32), 15)
        masks.append((diff == 15, diff == 0, diff == 1))
    for ox in range(3):
        for oy in range(3):
            at = 9 * ox + 3 * oy
            repeated = [kernel_ref[at + oz] for oz in range(3) for _ in range(4)]
            parts = contract_last(terms, jnp.concatenate(repeated, axis=0))
            both = parts[0:4] + parts[4:8] + parts[8:12]
            for q in range(4):
                low, mid, high = (
                    jnp.broadcast_to(both[q : q + 1, oz * 128 : oz * 128 + 128], (16, 128))
                    for oz in range(3)
                )
                for t in range(4):
                    below, same, above = masks[t]
                    piece = jnp.where(
                        same, mid, jnp.where(below, low, jnp.where(above, high, 0.0))
                    )
                    begin = oy * 256 + ox * 64 + q * 16
                    w0a_ref[begin : begin + 16, t * 128 : (t + 1) * 128] = piece.astype(bf16)
    for oy in range(3):
        w0a_ref[oy * 256 + 192 : oy * 256 + 256, :] = jnp.zeros((64, 512), bf16)


def bands(kernel_ref, out_ref, depth):
    group = iota((32, 128), 1) // 32
    zero = jnp.zeros((32, 128), f32)
    tiles = depth // 4

    def one(tap, carry):
        row = jnp.concatenate(
            [kernel_ref[3 * tap + oz].astype(f32) for oz in range(3)] + [zero[:, 0:32]], axis=1
        )
        turned = jnp.concatenate([row] * 4, axis=0).T
        low, mid, high = (turned[oz * 32 : oz * 32 + 32] for oz in range(3))

        def pick(*wanted):
            value = zero
            for index, piece in wanted:
                value = jnp.where(group == index, piece, value)
            return value

        patterns = (
            {0: pick((0, mid), (1, low)), -1: pick((3, high))},
            {0: pick((0, high), (1, mid), (2, low))},
            {0: pick((1, high), (2, mid), (3, low))},
            {0: pick((2, high), (3, mid)), 1: pick((0, low))},
        )
        for z in range(depth):
            content = {}
            for step, piece in patterns[z % 4].items():
                tile = (z // 4 + step) % tiles
                content[tile] = content[tile] + piece if tile in content else piece
            for tile in range(tiles):
                out_ref[tap, z * 32 : (z + 1) * 32, tile * 128 : (tile + 1) * 128] = (
                    content.get(tile, zero).astype(bf16)
                )
        return carry

    lax.fori_loop(0, 9, one, 0, unroll=3)


def middle_kernel(k1a_ref, k2_ref, after_ref, w1a_ref, w2_ref):
    bands(k1a_ref, w1a_ref, 8)
    bands(k2_ref, w2_ref, 4)


def last_kernel(
    head_ref, dest_ref, k1b_ref, k0b_ref, after_ref, w1b_ref, w0b_ref, headed_ref, rank_ref
):
    bands(k1b_ref, w1b_ref, 8)
    bands(k0b_ref, w0b_ref, 16)

    row16 = iota((16, 128), 0)
    names = head_ref[...].astype(f32)
    names = jnp.concatenate([names] * 4, axis=1)
    for t in range(4):
        same = row16 == 4 * t + iota((16, 128), 1) // 32
        rows = [
            jnp.where(same, jnp.broadcast_to(names[k : k + 1], (16, 128)), 0.0) for k in range(3)
        ]
        rows.append(jnp.zeros((80, 128), f32))
        headed_ref[t * 128 : t * 128 + 128, :] = jnp.concatenate(rows, axis=0).T.astype(bf16)

    dest = dest_ref[...]
    upper = (iota((128, 128), 0) <= iota((128, 128), 1)).astype(f32).astype(bf16)
    before = (iota((16, 16), 1) < iota((16, 16), 0)).astype(f32).astype(bf16)
    rank = jnp.zeros((16, 128), f32)
    for k in range(9):
        chosen = (dest == k).astype(f32)
        marks = chosen.astype(bf16)
        inside = dot(marks, upper)
        earlier = jnp.sum(dot(before, marks), axis=1, keepdims=True)
        rank = rank + chosen * (inside - 1.0 + earlier)
    rank_ref[...] = rank.astype(i32)


def in_vmem(kernel, shapes, values, after=()):
    vmem = pl.BlockSpec(memory_space=pltpu.VMEM)
    return pl.pallas_call(
        kernel,
        out_shape=tuple(pltpu.VMEM(shape, dtype) for shape, dtype in shapes),
        in_specs=[vmem] * len(values) + [pl.BlockSpec(memory_space=pl.ANY)] * len(after),
        out_specs=(vmem,) * len(shapes),
        compiler_params=pltpu.CompilerParams(vmem_limit_bytes=16 * 2**20),
        cost_estimate=pl.CostEstimate(
            flops=5_000_000, bytes_accessed=5_000_000, transcendentals=0
        ),
    )(*values, *after)


def lanes_of(ref):
    return jnp.concatenate([ref[chunk].astype(f32) for chunk in range(8)], axis=1)


def spread(value, taps_ref, targets):
    plain = value.astype(bf16)
    rolled = pltpu.roll(value, 2048 - 64, 1).astype(bf16)
    for column in range(COLS):
        if column % 2:
            piece = plain[:, 64 * (column + 1) : 64 * (column + 1) + 256]
        else:
            piece = rolled[:, 64 * column : 64 * column + 256]
        for oy, half in targets:
            begin = column * 32 + half * 16
            taps_ref[begin : begin + 16, oy * 256 : oy * 256 + 256] = piece


def first_conv(taps_ref, weight_ref, sums_ref, keep):
    for block in range(COLS // 4):
        value = gelu(dot(taps_ref[block * 128 : block * 128 + 128, :], weight_ref[...])).astype(bf16)
        keep(block, value)
        quads = value.astype(f32).reshape(2, 4, 16, 512)
        summed = (quads[:, 0] + quads[:, 1]) + (quads[:, 2] + quads[:, 3])
        sums_ref[block * 32 : block * 32 + 32, :] = summed.reshape(32, 512).astype(bf16)


def own_kernel(own_ref, w0a_ref, pool_ref, e0_ref, p1_ref, taps, sums):
    own = lanes_of(own_ref)
    even, odd = own[0:16], own[16:32]
    spread(pltpu.roll(odd, 1, 0), taps, ((0, 0),))
    spread(even, taps, ((0, 1), (1, 0)))
    spread(odd, taps, ((1, 1), (2, 0)))
    spread(pltpu.roll(even, 15, 0), taps, ((2, 1),))

    def keep(block, value):
        for column in range(4):
            n = block * 4 + column - 9
            if 0 <= n < 10:
                e0_ref[n * 32 : n * 32 + 32, :] = value[column * 32 : column * 32 + 32]

    first_conv(taps, w0a_ref, sums, keep)
    p1_ref[...] = dot(sums[...], pool_ref[...]).astype(bf16)


def own_part(own, w0a, pool):
    return pl.pallas_call(
        own_kernel,
        out_shape=(pltpu.VMEM((320, 512), bf16), pltpu.VMEM((224, 256), bf16)),
        scratch_shapes=[pltpu.VMEM((COLS * 32, 768), bf16), pltpu.VMEM((224, 512), bf16)],
        compiler_params=pltpu.CompilerParams(vmem_limit_bytes=16 * 2**20),
        cost_estimate=pl.CostEstimate(
            flops=2_000_000_000, bytes_accessed=2_000_000, transcendentals=500_000
        ),
    )(own, w0a, pool)


def network_kernel(
    own_ref,
    low_ref,
    high_ref,
    own_e0_ref,
    own_p1_ref,
    w0a_ref,
    w1a_ref,
    w2_ref,
    w1b_ref,
    w0b_ref,
    head_ref,
    pool_ref,
    grow_ref,
    pool1_ref,
    grow1_ref,
    rowpool_ref,
    rowgrow_ref,
    pos_ref,
    vel_ref,
    where_ref,
    dest_ref,
    rank_ref,
    out_ref,
    even,
    odd,
    taps,
    sums,
    e0_ref,
    p1_ref,
    p2_ref,
    u1_ref,
    ue_ref,
    uo_ref,
    um,
    u0,
    up,
):
    low = lanes_of(low_ref)
    high = lanes_of(high_ref)
    own = lanes_of(own_ref)
    for parity, ref in ((0, even), (1, odd)):
        ref[0:2, :] = jnp.zeros((2, 2048), f32)
        ref[2:8, :] = low[6 * parity : 6 * parity + 6]
        ref[8:24, :] = own[16 * parity : 16 * parity + 16]
        ref[24:30, :] = high[6 * parity : 6 * parity + 6]
        ref[30:32, :] = jnp.zeros((2, 2048), f32)

    def outer(ref, first):
        return jnp.concatenate([ref[first : first + 8, :], ref[first + 22 : first + 30, :]], axis=0)

    spread(outer(odd, 0), taps, ((0, 0),))
    spread(outer(even, 1), taps, ((0, 1), (1, 0)))
    spread(outer(odd, 1), taps, ((1, 1), (2, 0)))
    spread(outer(even, 2), taps, ((2, 1),))

    for n in range(10):
        for parity in range(2):
            at = n * 64 + parity * 32
            begin = n * 32 + parity * 16
            e0_ref[at + 8 : at + 24, :] = own_e0_ref[begin : begin + 16, :].astype(f32)

    def keep(block, value):
        for column in range(4):
            n = block * 4 + column - 9
            if 0 <= n < 10:
                for parity in range(2):
                    at = n * 64 + parity * 32
                    begin = column * 32 + parity * 16
                    rows = value[begin : begin + 16].astype(f32)
                    e0_ref[at + 1 : at + 9, :] = rows[0:8]
                    e0_ref[at + 23 : at + 31, :] = rows[8:16]

    first_conv(taps, w0a_ref, sums, keep)
    pooled = dot(sums[...], pool_ref[...]).astype(bf16).astype(f32)
    own_pooled = own_p1_ref[...].astype(f32)
    p1_ref[...] = jnp.zeros((464, 256), f32)
    for column in range(14):
        at = 8 + column * 32
        p1_ref[at + 8 : at + 24, :] = own_pooled[column * 16 : column * 16 + 16]
        p1_ref[at + 1 : at + 9, :] = pooled[column * 16 : column * 16 + 8]
        p1_ref[at + 23 : at + 31, :] = pooled[column * 16 + 8 : column * 16 + 16]

    def middle(ref, blocks, weight_ref, stride, size, pad):
        shifted = [ref[pad + oy - 1 : pad + oy - 1 + size, :].astype(bf16) for oy in range(3)]
        total = None
        for ox in range(3):
            for oy in range(3):
                piece = shifted[oy][ox * stride : ox * stride + blocks * stride]
                term = dot(piece, weight_ref[ox * 3 + oy])
                total = term if total is None else total + term
        return gelu(total).astype(bf16)

    e1 = middle(p1_ref, 12, w1a_ref, 32, 448, 8)
    part = dot(rowpool_ref[...], e1).astype(bf16)
    p2_ref[0:8, :] = jnp.zeros((8, 128), f32)
    p2_ref[104:112, :] = jnp.zeros((8, 128), f32)
    p2_ref[8:104, :] = dot(part, pool1_ref[...]).astype(bf16).astype(f32)
    e2 = middle(p2_ref, 4, w2_ref, 16, 96, 8)
    grown = dot(dot(rowgrow_ref[...], e2).astype(bf16), grow1_ref[...])
    u1_ref[0:8, :] = jnp.zeros((8, 256), f32)
    u1_ref[264:272, :] = jnp.zeros((8, 256), f32)
    u1_ref[8:264, :] = (e1[64:320].astype(f32) + grown).astype(bf16).astype(f32)
    f1 = middle(u1_ref, 6, w1b_ref, 32, 256, 8)
    grown = dot(f1, grow_ref[...])
    for n in range(10):
        add = grown[((n + 1) // 2) * 32 : ((n + 1) // 2) * 32 + 32]
        begin = n * 64
        ue_ref[...] = (e0_ref[begin : begin + 32, :] + add).astype(bf16).astype(f32)
        uo_ref[...] = (e0_ref[begin + 32 : begin + 64, :] + add).astype(bf16).astype(f32)
        at = n * 32
        even_here = ue_ref[8:24, :].astype(bf16)
        odd_here = uo_ref[8:24, :].astype(bf16)
        um[at : at + 16, :] = uo_ref[7:23, :].astype(bf16)
        um[at + 16 : at + 32, :] = even_here
        u0[at : at + 16, :] = even_here
        u0[at + 16 : at + 32, :] = odd_here
        up[at : at + 16, :] = odd_here
        up[at + 16 : at + 32, :] = ue_ref[9:25, :].astype(bf16)

    total = None
    for ox in range(3):
        for oy, ref in enumerate((um, u0, up)):
            term = dot(ref[ox * 32 : ox * 32 + 256, :], w0b_ref[ox * 3 + oy])
            total = term if total is None else total + term
    change = dot(gelu(total).astype(bf16), head_ref[...])

    lane16 = iota((32, 128), 1) // 16
    tables = []
    for comp in range(3):
        table = jnp.zeros((32, 128), f32)
        for x in range(8):
            block = change[x * 32 : x * 32 + 32]
            shift = ((x - comp) * 16) % 128
            moved = pltpu.roll(block, shift, 1) if shift else block
            table = jnp.where(lane16 == x, moved, table)
        tables.append(table)
    cell = where_ref[...]
    y = jnp.bitwise_and(jnp.right_shift(cell, 4), 31)
    row = jnp.bitwise_and(y, 1) * 16 + jnp.right_shift(y, 1)
    lane = jnp.right_shift(cell, 9) * 16 + jnp.bitwise_and(cell, 15)
    kick = [jnp.zeros((16, 128), f32) for _ in range(3)]
    for r in range(32):
        here = row == r
        for comp in range(3):
            source = jnp.broadcast_to(tables[comp][r : r + 1], (16, 128))
            kick[comp] = jnp.where(here, pick_lanes(source, lane), kick[comp])
    payload = []
    speeds = [vel_ref[comp] + kick[comp] for comp in range(3)]
    for comp in range(3):
        payload.append(pos_ref[comp] + DRIFT * speeds[comp])
    payload = payload + speeds

    rank = rank_ref[...]
    key = dest_ref[...] * 4 + jnp.right_shift(rank, 7)
    slot = jnp.bitwise_and(rank, 127)
    line = iota((216, 128), 0)
    line_key = (line // 24) * 4 + jnp.bitwise_and(line, 3)
    slots = iota((128, 128), 0)
    packed = jnp.zeros((216, 128), f32)
    for pair in range(8):
        left, right = [], []
        for c in (2 * pair, 2 * pair + 1):
            rows = jnp.concatenate(
                [jnp.broadcast_to(part[c : c + 1], (4, 128)) for part in payload], axis=0
            )
            full = jnp.concatenate([rows] * 9, axis=0)
            left.append(jnp.where(line_key == key[c : c + 1], full, 0.0).astype(bf16))
            right.append((slots == slot[c : c + 1]).astype(f32).astype(bf16))
        packed = packed + contract_last(
            jnp.concatenate(left, axis=1), jnp.concatenate(right, axis=1)
        )
    out_ref[...] = packed.astype(bf16)


def constants():
    pool = np.zeros((NZ * CH, NZ // 2 * CH), np.float32)
    for z in range(NZ):
        for c in range(CH):
            pool[z * CH + c, z // 2 * CH + c] = 1.0
    pool1 = pool[: 8 * CH, : 4 * CH]
    rowpool = np.zeros((96, 384), np.float32)
    for a in range(6):
        for s in range(12):
            for dx in range(2):
                for dy in range(2):
                    rowpool[a * 16 + s, (2 * a + dx) * 32 + 2 * s + 4 + dy] = 0.25
    rowgrow = np.zeros((256, 64), np.float32)
    for c in range(8):
        for r in range(6, 26):
            rowgrow[c * 32 + r, (c // 2) * 16 + (r - 4) // 2] = 1.0
    made = (pool * 0.125, pool.T, pool1 * 0.5, pool1.T, rowpool, rowgrow)
    return [jnp.asarray(np.ascontiguousarray(value), bf16) for value in made]


def network(own, low, high, fine, weights, head, fixed, pos, vel, where, dest, rank):
    vmem = pl.BlockSpec(memory_space=pltpu.VMEM)
    return pl.pallas_call(
        network_kernel,
        out_shape=pltpu.VMEM((216, 128), bf16),
        in_specs=[vmem] * 22,
        out_specs=vmem,
        scratch_shapes=[
            pltpu.VMEM((32, 2048), f32),
            pltpu.VMEM((32, 2048), f32),
            pltpu.VMEM((COLS * 32, 768), bf16),
            pltpu.VMEM((224, 512), bf16),
            pltpu.VMEM((640, 512), f32),
            pltpu.VMEM((464, 256), f32),
            pltpu.VMEM((112, 128), f32),
            pltpu.VMEM((272, 256), f32),
            pltpu.VMEM((32, 512), f32),
            pltpu.VMEM((32, 512), f32),
            pltpu.VMEM((320, 512), bf16),
            pltpu.VMEM((320, 512), bf16),
            pltpu.VMEM((320, 512), bf16),
        ],
        compiler_params=pltpu.CompilerParams(vmem_limit_bytes=36 * 2**20),
        cost_estimate=pl.CostEstimate(
            flops=3_000_000_000, bytes_accessed=10_000_000, transcendentals=1_000_000
        ),
    )(own, low, high, *fine, *weights, head, *fixed, pos, vel, where, dest, rank)


def exchange(value, count_x, count_y, rule):
    pairs = []
    for i in range(count_x):
        for j in range(count_y):
            a, b = rule(i, j)
            pairs.append((i * count_y + j, (a % count_x) * count_y + b % count_y))
    return lax.ppermute(value, ("gx", "gy"), pairs)


def body(
    position,
    velocity,
    cell_list,
    slot_weight,
    particle_cell,
    destination,
    lift,
    kernel_0a,
    kernel_1a,
    kernel_2,
    kernel_1b,
    kernel_0b,
    head,
):
    count_x, count_y = lax.axis_size("gx"), lax.axis_size("gy")
    first_core = lax.rem(lax.axis_index("gx"), 2) == 0

    def mate(value):
        return exchange(value, count_x, count_y, lambda i, j: (i ^ 1, j))

    def cross(value):
        return exchange(value, count_x, count_y, lambda i, j: (i + 1 if i % 2 else i - 1, j))

    def along_y(value):
        return exchange(value, count_x, count_y, lambda i, j: (i, j - 1 if i % 2 else j + 1))

    def either(if_first, if_second):
        return jnp.where(first_core, if_first, if_second)

    def cat(parts, axis):
        return jnp.concatenate(parts, axis=axis)

    def barrier(*values):
        return lax.optimization_barrier(values)

    fixed = constants()
    dest = destination.reshape(16, 128)

    raw = (kernel_0a, lift.T, kernel_1a, kernel_2, kernel_1b, kernel_0b, head, dest)
    mine, *raw = deposit(velocity, cell_list, slot_weight, raw)
    kernel_0a, lifting, kernel_1a, kernel_2, kernel_1b, kernel_0b, head, dest = raw
    theirs = mate(mine)
    near = cross(cat([mine, either(theirs[0:1], theirs[1:2])], 0))
    chip = cat([either(mine, theirs), either(theirs, mine)], 0)

    (w0a,) = in_vmem(first_kernel, [((768, 512), bf16)], (lifting, kernel_0a))
    w1a, w2 = in_vmem(
        middle_kernel,
        [((9, 256, 256), bf16), ((9, 128, 128), bf16)],
        (kernel_1a, kernel_2),
        (theirs,),
    )
    near, w0a, w1a, w2 = barrier(near, w0a, w1a, w2)
    far = mate(near)
    left, right = either(near, far), either(far, near)
    wide = cat([left[2:3], left[0:2], chip, right], 0)
    near = along_y(
        either(
            cat([wide[:, 10:16], wide[:, 26:32]], 1), cat([wide[:, 0:6], wide[:, 16:22]], 1)
        )
    )
    own = either(wide[0:8], wide[2:10])
    fine = own_part(own, w0a, fixed[0])
    w1b, w0b, headed, rank = in_vmem(
        last_kernel,
        [((9, 256, 256), bf16), ((9, 512, 512), bf16), ((512, 128), bf16), ((16, 128), i32)],
        (head, dest, kernel_1b, kernel_0b),
        (own,),
    )
    weights = (w0a, w1a, w2, w1b, w0b)
    near, fine, weights, headed, rank = barrier(near, fine, weights, headed, rank)
    far = mate(either(near[2:10], near[0:8]))
    near = either(near[0:8], near[2:10])
    low, high = either(near, far), either(far, near)

    packed = network(
        own,
        low,
        high,
        fine,
        weights,
        headed,
        fixed,
        position.reshape(3, 16, 128),
        velocity.reshape(3, 16, 128),
        particle_cell.reshape(16, 128),
        dest,
        rank,
    )

    behind, level, ahead = packed[0:72], packed[72:144], packed[144:216]
    from_mate = mate(either(ahead, behind))
    from_cross = cross(either(behind, ahead))
    behind = either(from_mate, from_cross)
    ahead = either(from_cross, from_mate)
    groups = (behind, level, ahead)
    down = cat([group[0:24] for group in groups], 0)
    upward = cat([group[48:72] for group in groups], 0)
    passed = mate(either(down, upward))
    near = along_y(cat([either(upward, down), passed], 0))
    far = mate(near[72:])
    near = near[:72]
    upward, down = either(near, far), either(far, near)
    blocks = []
    for a in range(3):
        blocks.append(down[24 * a : 24 * a + 24])
        blocks.append(groups[a][24:48])
        blocks.append(upward[24 * a : 24 * a + 24])
    inbox = jnp.stack(blocks, axis=0).reshape(9, 6, CAP)
    return inbox.astype(f32).transpose(1, 0, 2).reshape(6, 9 * CAP)


def solution(mesh):
    in_specs = (
        P(None, ("gx", "gy")),
        P(None, ("gx", "gy")),
        P(None, "gx", "gy", None),
        P(None, "gx", "gy", None),
        P(("gx", "gy")),
        P(("gx", "gy"), None),
        P(),
        P(),
        P(),
        P(),
        P(),
        P(),
        P(),
    )
    out_specs = P(None, ("gx", "gy"))
    return jax.shard_map(body, mesh=mesh, in_specs=in_specs, out_specs=out_specs, check_vma=False)
```

```python
import jax
import jax.numpy as jnp
import numpy as np
from jax import lax
from jax.experimental import pallas as pl
from jax.experimental.pallas import tpu as pltpu
from jax.sharding import PartitionSpec as P

f32 = jnp.float32
bf16 = jnp.bfloat16
i32 = jnp.int32

CAP = 512
DRIFT = 0.25
CH = 32
NZ = 16
COLS = 28


def iota(shape, dim):
    return lax.broadcasted_iota(i32, shape, dim)


def dot(a, b):
    return jnp.dot(a, b, preferred_element_type=f32)


def gelu(x):
    inner = x * (0.7978845608028654 + 0.035677408136300125 * (x * x))
    return (0.5 * x) * (1.0 + jnp.tanh(inner))


def pick_lanes(table, lane):
    numbers = lax.GatherDimensionNumbers(
        offset_dims=(),
        collapsed_slice_dims=(1,),
        start_index_map=(1,),
        operand_batching_dims=(0,),
        start_indices_batching_dims=(0,),
    )
    return lax.gather(
        table,
        lane[..., None],
        numbers,
        (1, 1),
        mode=lax.GatherScatterMode.PROMISE_IN_BOUNDS,
    )


def fetch_all(pairs, sems):
    copies = [
        pltpu.make_async_copy(source, target, sems.at[index])
        for index, (source, target) in enumerate(pairs)
    ]
    for copy in copies:
        copy.start()
    return copies


def deposit_kernel(*refs):
    vel_hbm, cells_hbm, weight_hbm = refs[:3]
    raw_in, out_ref, raw_out = refs[3:11], refs[11], refs[12:20]
    stage, vel_ref, cells_ref, weight_ref, sems, raw_sems = refs[20:]
    fetch_vel, fetch_cells, fetch_weight = fetch_all(
        ((vel_hbm, vel_ref), (cells_hbm, cells_ref), (weight_hbm, weight_ref)), sems
    )
    raw_fetches = fetch_all(zip(raw_in, raw_out), raw_sems)

    def dense(ref, s):
        return jnp.concatenate(
            [jnp.concatenate([ref[s, 2 * a + b] for a in range(4)], axis=1) for b in range(2)],
            axis=0,
        )

    fetch_vel.wait()
    fetch_cells.wait()
    entries = [dense(cells_ref, s) for s in range(4)]
    tables = [
        [
            jnp.broadcast_to(vel_ref[q : q + 1, r * 128 : (r + 1) * 128], (8, 128))
            for q in range(3)
        ]
        for r in range(16)
    ]
    picked = []
    for s in range(4):
        pieces = [[], [], []]
        for begin in range(0, 32, 8):
            entry = entries[s][begin : begin + 8]
            lane = jnp.bitwise_and(entry, 127)
            row = jnp.right_shift(entry, 7)
            found = [jnp.zeros((8, 128), f32) for _ in range(3)]
            for r in range(16):
                here = row == r
                for q in range(3):
                    found[q] = jnp.where(here, pick_lanes(tables[r][q], lane), found[q])
            for q in range(3):
                pieces[q].append(found[q])
        picked.append([jnp.concatenate(piece, axis=0) for piece in pieces])
    fetch_weight.wait()
    totals = [jnp.zeros((32, 128), f32) for _ in range(4)]
    for s in range(4):
        weight = dense(weight_ref, s)
        totals[0] = totals[0] + jnp.where(entries[s] < 2048, weight, 0.0)
        for q in range(3):
            totals[q + 1] = totals[q + 1] + weight * picked[s][q]
    stage[...] = jnp.concatenate(
        [totals[q][b * 16 : b * 16 + 16] for b in range(2) for q in range(4)], axis=0
    ).T
    for t in range(4):
        for parity in range(2):
            lanes = slice((t % 2) * 128, (t % 2) * 128 + 128)
            out_ref[t // 2, parity * 16 : parity * 16 + 16, lanes] = stage[
                pl.ds(t * 32 + parity, 16, stride=2), :
            ].astype(bf16)
    for fetch in raw_fetches:
        fetch.wait()


def deposit(velocity, cells, weight, raw):
    return pl.pallas_call(
        deposit_kernel,
        out_shape=(
            pltpu.VMEM((2, 32, 256), bf16),
            *(pltpu.VMEM(value.shape, value.dtype) for value in raw),
        ),
        in_specs=[pl.BlockSpec(memory_space=pltpu.HBM)] * 11,
        out_specs=[pl.BlockSpec(memory_space=pltpu.VMEM)] * 9,
        scratch_shapes=[
            pltpu.VMEM((128, 128), f32),
            pltpu.VMEM((3, 2048), f32),
            pltpu.VMEM((4, 8, 16, 32), i32),
            pltpu.VMEM((4, 8, 16, 32), f32),
            pltpu.SemaphoreType.DMA((3,)),
            pltpu.SemaphoreType.DMA((8,)),
        ],
        cost_estimate=pl.CostEstimate(flops=2_000_000, bytes_accessed=1_000_000, transcendentals=0),
    )(velocity, jnp.swapaxes(cells, 2, 3), jnp.swapaxes(weight, 2, 3), *raw)


def contract_last(a, b):
    return lax.dot_general(a, b, (((1,), (1,)), ((), ())), preferred_element_type=f32)


def first_kernel(lift_ref, kernel_ref, w0a_ref):
    rest = lift_ref[...]
    terms = []
    for _ in range(3):
        term = rest.astype(bf16).astype(f32)
        terms.append(term)
        rest = rest - term
    terms = jnp.concatenate(terms + [jnp.zeros((4, 32), f32)], axis=0).astype(bf16)
    row = iota((16, 128), 0)
    masks = []
    for t in range(4):
        diff = jnp.bitwise_and(row - (4 * t + iota((16, 128), 1) // 32), 15)
        masks.append((diff == 15, diff == 0, diff == 1))
    for ox in range(3):
        for oy in range(3):
            at = 9 * ox + 3 * oy
            repeated = [kernel_ref[at + oz] for oz in range(3) for _ in range(4)]
            parts = contract_last(terms, jnp.concatenate(repeated, axis=0))
            both = parts[0:4] + parts[4:8] + parts[8:12]
            for q in range(4):
                low, mid, high = (
                    jnp.broadcast_to(both[q : q + 1, oz * 128 : oz * 128 + 128], (16, 128))
                    for oz in range(3)
                )
                for t in range(4):
                    below, same, above = masks[t]
                    piece = jnp.where(
                        same, mid, jnp.where(below, low, jnp.where(above, high, 0.0))
                    )
                    begin = oy * 256 + ox * 64 + q * 16
                    w0a_ref[begin : begin + 16, t * 128 : (t + 1) * 128] = piece.astype(bf16)
    for oy in range(3):
        w0a_ref[oy * 256 + 192 : oy * 256 + 256, :] = jnp.zeros((64, 512), bf16)


def bands(kernel_ref, out_ref, depth):
    group = iota((32, 128), 1) // 32
    zero = jnp.zeros((32, 128), f32)
    tiles = depth // 4

    def one(tap, carry):
        row = jnp.concatenate(
            [kernel_ref[3 * tap + oz].astype(f32) for oz in range(3)] + [zero[:, 0:32]], axis=1
        )
        turned = jnp.concatenate([row] * 4, axis=0).T
        low, mid, high = (turned[oz * 32 : oz * 32 + 32] for oz in range(3))

        def pick(*wanted):
            value = zero
            for index, piece in wanted:
                value = jnp.where(group == index, piece, value)
            return value

        patterns = (
            {0: pick((0, mid), (1, low)), -1: pick((3, high))},
            {0: pick((0, high), (1, mid), (2, low))},
            {0: pick((1, high), (2, mid), (3, low))},
            {0: pick((2, high), (3, mid)), 1: pick((0, low))},
        )
        for z in range(depth):
            content = {}
            for step, piece in patterns[z % 4].items():
                tile = (z // 4 + step) % tiles
                content[tile] = content[tile] + piece if tile in content else piece
            for tile in range(tiles):
                out_ref[tap, z * 32 : (z + 1) * 32, tile * 128 : (tile + 1) * 128] = (
                    content.get(tile, zero).astype(bf16)
                )
        return carry

    lax.fori_loop(0, 9, one, 0, unroll=3)


def middle_kernel(k1a_ref, k2_ref, after_ref, w1a_ref, w2_ref):
    bands(k1a_ref, w1a_ref, 8)
    bands(k2_ref, w2_ref, 4)


def last_kernel(
    head_ref, dest_ref, k1b_ref, k0b_ref, after_ref, w1b_ref, w0b_ref, headed_ref, rank_ref
):
    bands(k1b_ref, w1b_ref, 8)
    bands(k0b_ref, w0b_ref, 16)

    row16 = iota((16, 128), 0)
    names = head_ref[...].astype(f32)
    names = jnp.concatenate([names] * 4, axis=1)
    for t in range(4):
        same = row16 == 4 * t + iota((16, 128), 1) // 32
        rows = [
            jnp.where(same, jnp.broadcast_to(names[k : k + 1], (16, 128)), 0.0) for k in range(3)
        ]
        rows.append(jnp.zeros((80, 128), f32))
        headed_ref[t * 128 : t * 128 + 128, :] = jnp.concatenate(rows, axis=0).T.astype(bf16)

    dest = dest_ref[...]
    upper = (iota((128, 128), 0) <= iota((128, 128), 1)).astype(f32).astype(bf16)
    before = (iota((16, 16), 1) < iota((16, 16), 0)).astype(f32).astype(bf16)
    rank = jnp.zeros((16, 128), f32)
    for k in range(9):
        chosen = (dest == k).astype(f32)
        marks = chosen.astype(bf16)
        inside = dot(marks, upper)
        earlier = jnp.sum(dot(before, marks), axis=1, keepdims=True)
        rank = rank + chosen * (inside - 1.0 + earlier)
    rank_ref[...] = rank.astype(i32)


def in_vmem(kernel, shapes, values, after=()):
    vmem = pl.BlockSpec(memory_space=pltpu.VMEM)
    return pl.pallas_call(
        kernel,
        out_shape=tuple(pltpu.VMEM(shape, dtype) for shape, dtype in shapes),
        in_specs=[vmem] * len(values) + [pl.BlockSpec(memory_space=pl.ANY)] * len(after),
        out_specs=(vmem,) * len(shapes),
        compiler_params=pltpu.CompilerParams(vmem_limit_bytes=16 * 2**20),
        cost_estimate=pl.CostEstimate(
            flops=5_000_000, bytes_accessed=5_000_000, transcendentals=0
        ),
    )(*values, *after)


def lanes_of(ref):
    return jnp.concatenate([ref[chunk].astype(f32) for chunk in range(8)], axis=1)


def spread(value, taps_ref, targets):
    plain = value.astype(bf16)
    rolled = pltpu.roll(value, 2048 - 64, 1).astype(bf16)
    for column in range(COLS):
        if column % 2:
            piece = plain[:, 64 * (column + 1) : 64 * (column + 1) + 256]
        else:
            piece = rolled[:, 64 * column : 64 * column + 256]
        for oy, half in targets:
            begin = column * 32 + half * 16
            taps_ref[begin : begin + 16, oy * 256 : oy * 256 + 256] = piece


def first_conv(taps_ref, weight_ref, sums_ref, keep):
    for block in range(COLS // 4):
        value = gelu(dot(taps_ref[block * 128 : block * 128 + 128, :], weight_ref[...])).astype(bf16)
        keep(block, value)
        quads = value.astype(f32).reshape(2, 4, 16, 512)
        summed = (quads[:, 0] + quads[:, 1]) + (quads[:, 2] + quads[:, 3])
        sums_ref[block * 32 : block * 32 + 32, :] = summed.reshape(32, 512).astype(bf16)


def own_kernel(own_ref, w0a_ref, pool_ref, e0_ref, p1_ref, taps, sums):
    own = lanes_of(own_ref)
    even, odd = own[0:16], own[16:32]
    spread(pltpu.roll(odd, 1, 0), taps, ((0, 0),))
    spread(even, taps, ((0, 1), (1, 0)))
    spread(odd, taps, ((1, 1), (2, 0)))
    spread(pltpu.roll(even, 15, 0), taps, ((2, 1),))

    def keep(block, value):
        for column in range(4):
            n = block * 4 + column - 9
            if 0 <= n < 10:
                e0_ref[n * 32 : n * 32 + 32, :] = value[column * 32 : column * 32 + 32]

    first_conv(taps, w0a_ref, sums, keep)
    p1_ref[...] = dot(sums[...], pool_ref[...]).astype(bf16)


def own_part(own, w0a, pool):
    return pl.pallas_call(
        own_kernel,
        out_shape=(pltpu.VMEM((320, 512), bf16), pltpu.VMEM((224, 256), bf16)),
        scratch_shapes=[pltpu.VMEM((COLS * 32, 768), bf16), pltpu.VMEM((224, 512), bf16)],
        compiler_params=pltpu.CompilerParams(vmem_limit_bytes=16 * 2**20),
        cost_estimate=pl.CostEstimate(
            flops=2_000_000_000, bytes_accessed=2_000_000, transcendentals=500_000
        ),
    )(own, w0a, pool)


def network_kernel(
    own_ref,
    low_ref,
    high_ref,
    own_e0_ref,
    own_p1_ref,
    w0a_ref,
    w1a_ref,
    w2_ref,
    w1b_ref,
    w0b_ref,
    head_ref,
    pool_ref,
    grow_ref,
    pool1_ref,
    grow1_ref,
    rowpool_ref,
    rowgrow_ref,
    pos_ref,
    vel_ref,
    where_ref,
    dest_ref,
    rank_ref,
    out_ref,
    even,
    odd,
    taps,
    sums,
    e0_ref,
    p1_ref,
    p2_ref,
    u1_ref,
    ue_ref,
    uo_ref,
    um,
    u0,
    up,
):
    low = lanes_of(low_ref)
    high = lanes_of(high_ref)
    own = lanes_of(own_ref)
    for parity, ref in ((0, even), (1, odd)):
        ref[0:2, :] = jnp.zeros((2, 2048), f32)
        ref[2:8, :] = low[6 * parity : 6 * parity + 6]
        ref[8:24, :] = own[16 * parity : 16 * parity + 16]
        ref[24:30, :] = high[6 * parity : 6 * parity + 6]
        ref[30:32, :] = jnp.zeros((2, 2048), f32)

    def outer(ref, first):
        return jnp.concatenate([ref[first : first + 8, :], ref[first + 22 : first + 30, :]], axis=0)

    spread(outer(odd, 0), taps, ((0, 0),))
    spread(outer(even, 1), taps, ((0, 1), (1, 0)))
    spread(outer(odd, 1), taps, ((1, 1), (2, 0)))
    spread(outer(even, 2), taps, ((2, 1),))

    for n in range(10):
        for parity in range(2):
            at = n * 64 + parity * 32
            begin = n * 32 + parity * 16
            e0_ref[at + 8 : at + 24, :] = own_e0_ref[begin : begin + 16, :].astype(f32)

    def keep(block, value):
        for column in range(4):
            n = block * 4 + column - 9
            if 0 <= n < 10:
                for parity in range(2):
                    at = n * 64 + parity * 32
                    begin = column * 32 + parity * 16
                    rows = value[begin : begin + 16].astype(f32)
                    e0_ref[at + 1 : at + 9, :] = rows[0:8]
                    e0_ref[at + 23 : at + 31, :] = rows[8:16]

    first_conv(taps, w0a_ref, sums, keep)
    pooled = dot(sums[...], pool_ref[...]).astype(bf16).astype(f32)
    own_pooled = own_p1_ref[...].astype(f32)
    p1_ref[...] = jnp.zeros((464, 256), f32)
    for column in range(14):
        at = 8 + column * 32
        p1_ref[at + 8 : at + 24, :] = own_pooled[column * 16 : column * 16 + 16]
        p1_ref[at + 1 : at + 9, :] = pooled[column * 16 : column * 16 + 8]
        p1_ref[at + 23 : at + 31, :] = pooled[column * 16 + 8 : column * 16 + 16]

    def middle(ref, blocks, weight_ref, stride, size, pad):
        shifted = [ref[pad + oy - 1 : pad + oy - 1 + size, :].astype(bf16) for oy in range(3)]
        pieces = [
            shifted[oy][ox * stride : ox * stride + blocks * stride]
            for ox in range(3)
            for oy in range(3)
        ]
        width = weight_ref.shape[2]
        total = dot(jnp.concatenate(pieces, axis=1), weight_ref[...].reshape(9 * width, width))
        return gelu(total).astype(bf16)

    e1 = middle(p1_ref, 12, w1a_ref, 32, 448, 8)
    part = dot(rowpool_ref[...], e1).astype(bf16)
    p2_ref[0:8, :] = jnp.zeros((8, 128), f32)
    p2_ref[104:112, :] = jnp.zeros((8, 128), f32)
    p2_ref[8:104, :] = dot(part, pool1_ref[...]).astype(bf16).astype(f32)
    e2 = middle(p2_ref, 4, w2_ref, 16, 96, 8)
    grown = dot(dot(rowgrow_ref[...], e2).astype(bf16), grow1_ref[...])
    u1_ref[0:8, :] = jnp.zeros((8, 256), f32)
    u1_ref[264:272, :] = jnp.zeros((8, 256), f32)
    u1_ref[8:264, :] = (e1[64:320].astype(f32) + grown).astype(bf16).astype(f32)
    f1 = middle(u1_ref, 6, w1b_ref, 32, 256, 8)
    grown = dot(f1, grow_ref[...])
    for n in range(10):
        add = grown[((n + 1) // 2) * 32 : ((n + 1) // 2) * 32 + 32]
        begin = n * 64
        ue_ref[...] = (e0_ref[begin : begin + 32, :] + add).astype(bf16).astype(f32)
        uo_ref[...] = (e0_ref[begin + 32 : begin + 64, :] + add).astype(bf16).astype(f32)
        at = n * 32
        even_here = ue_ref[8:24, :].astype(bf16)
        odd_here = uo_ref[8:24, :].astype(bf16)
        um[at : at + 16, :] = uo_ref[7:23, :].astype(bf16)
        um[at + 16 : at + 32, :] = even_here
        u0[at : at + 16, :] = even_here
        u0[at + 16 : at + 32, :] = odd_here
        up[at : at + 16, :] = odd_here
        up[at + 16 : at + 32, :] = ue_ref[9:25, :].astype(bf16)

    pieces = [ref[ox * 32 : ox * 32 + 256, :] for ox in range(3) for ref in (um, u0, up)]
    total = dot(jnp.concatenate(pieces, axis=1), w0b_ref[...].reshape(9 * 512, 512))
    change = dot(gelu(total).astype(bf16), head_ref[...])

    lane16 = iota((32, 128), 1) // 16
    tables = []
    for comp in range(3):
        table = jnp.zeros((32, 128), f32)
        for x in range(8):
            block = change[x * 32 : x * 32 + 32]
            shift = ((x - comp) * 16) % 128
            moved = pltpu.roll(block, shift, 1) if shift else block
            table = jnp.where(lane16 == x, moved, table)
        tables.append(table)
    cell = where_ref[...]
    y = jnp.bitwise_and(jnp.right_shift(cell, 4), 31)
    row = jnp.bitwise_and(y, 1) * 16 + jnp.right_shift(y, 1)
    lane = jnp.right_shift(cell, 9) * 16 + jnp.bitwise_and(cell, 15)
    pieces = [[], [], []]
    for begin in (0, 8):
        row_here, lane_here = row[begin : begin + 8], lane[begin : begin + 8]
        found = [jnp.zeros((8, 128), f32) for _ in range(3)]
        for r in range(32):
            here = row_here == r
            for comp in range(3):
                source = jnp.broadcast_to(tables[comp][r : r + 1], (8, 128))
                found[comp] = jnp.where(here, pick_lanes(source, lane_here), found[comp])
        for comp in range(3):
            pieces[comp].append(found[comp])
    kick = [jnp.concatenate(piece, axis=0) for piece in pieces]
    payload = []
    speeds = [vel_ref[comp] + kick[comp] for comp in range(3)]
    for comp in range(3):
        payload.append(pos_ref[comp] + DRIFT * speeds[comp])
    payload = payload + speeds

    rank = rank_ref[...]
    key = dest_ref[...] * 4 + jnp.right_shift(rank, 7)
    slot = jnp.bitwise_and(rank, 127)
    line = iota((216, 128), 0)
    line_key = (line // 24) * 4 + jnp.bitwise_and(line, 3)
    slots = iota((128, 128), 0)
    packed = jnp.zeros((216, 128), f32)
    for pair in range(8):
        left, right = [], []
        for c in (2 * pair, 2 * pair + 1):
            rows = jnp.concatenate(
                [jnp.broadcast_to(part[c : c + 1], (4, 128)) for part in payload], axis=0
            )
            full = jnp.concatenate([rows] * 9, axis=0)
            left.append(jnp.where(line_key == key[c : c + 1], full, 0.0).astype(bf16))
            right.append((slots == slot[c : c + 1]).astype(f32).astype(bf16))
        packed = packed + contract_last(
            jnp.concatenate(left, axis=1), jnp.concatenate(right, axis=1)
        )
    out_ref[...] = packed.astype(bf16)


def constants():
    pool = np.zeros((NZ * CH, NZ // 2 * CH), np.float32)
    for z in range(NZ):
        for c in range(CH):
            pool[z * CH + c, z // 2 * CH + c] = 1.0
    pool1 = pool[: 8 * CH, : 4 * CH]
    rowpool = np.zeros((96, 384), np.float32)
    for a in range(6):
        for s in range(12):
            for dx in range(2):
                for dy in range(2):
                    rowpool[a * 16 + s, (2 * a + dx) * 32 + 2 * s + 4 + dy] = 0.25
    rowgrow = np.zeros((256, 64), np.float32)
    for c in range(8):
        for r in range(6, 26):
            rowgrow[c * 32 + r, (c // 2) * 16 + (r - 4) // 2] = 1.0
    made = (pool * 0.125, pool.T, pool1 * 0.5, pool1.T, rowpool, rowgrow)
    return [jnp.asarray(np.ascontiguousarray(value), bf16) for value in made]


def network(own, low, high, fine, weights, head, fixed, pos, vel, where, dest, rank):
    vmem = pl.BlockSpec(memory_space=pltpu.VMEM)
    return pl.pallas_call(
        network_kernel,
        out_shape=pltpu.VMEM((216, 128), bf16),
        in_specs=[vmem] * 22,
        out_specs=vmem,
        scratch_shapes=[
            pltpu.VMEM((32, 2048), f32),
            pltpu.VMEM((32, 2048), f32),
            pltpu.VMEM((COLS * 32, 768), bf16),
            pltpu.VMEM((224, 512), bf16),
            pltpu.VMEM((640, 512), f32),
            pltpu.VMEM((464, 256), f32),
            pltpu.VMEM((112, 128), f32),
            pltpu.VMEM((272, 256), f32),
            pltpu.VMEM((32, 512), f32),
            pltpu.VMEM((32, 512), f32),
            pltpu.VMEM((320, 512), bf16),
            pltpu.VMEM((320, 512), bf16),
            pltpu.VMEM((320, 512), bf16),
        ],
        compiler_params=pltpu.CompilerParams(vmem_limit_bytes=36 * 2**20),
        cost_estimate=pl.CostEstimate(
            flops=3_000_000_000, bytes_accessed=10_000_000, transcendentals=1_000_000
        ),
    )(own, low, high, *fine, *weights, head, *fixed, pos, vel, where, dest, rank)


def exchange(value, count_x, count_y, rule):
    pairs = []
    for i in range(count_x):
        for j in range(count_y):
            a, b = rule(i, j)
            pairs.append((i * count_y + j, (a % count_x) * count_y + b % count_y))
    return lax.ppermute(value, ("gx", "gy"), pairs)


def body(
    position,
    velocity,
    cell_list,
    slot_weight,
    particle_cell,
    destination,
    lift,
    kernel_0a,
    kernel_1a,
    kernel_2,
    kernel_1b,
    kernel_0b,
    head,
):
    count_x, count_y = lax.axis_size("gx"), lax.axis_size("gy")
    first_core = lax.rem(lax.axis_index("gx"), 2) == 0

    def mate(value):
        return exchange(value, count_x, count_y, lambda i, j: (i ^ 1, j))

    def cross(value):
        return exchange(value, count_x, count_y, lambda i, j: (i + 1 if i % 2 else i - 1, j))

    def along_y(value):
        return exchange(value, count_x, count_y, lambda i, j: (i, j - 1 if i % 2 else j + 1))

    def along(value, step):
        return exchange(value, count_x, count_y, lambda i, j: (i, j + step))

    def either(if_first, if_second):
        return jnp.where(first_core, if_first, if_second)

    def cat(parts, axis):
        return jnp.concatenate(parts, axis=axis)

    def barrier(*values):
        return lax.optimization_barrier(values)

    fixed = constants()
    dest = destination.reshape(16, 128)

    raw = (kernel_0a, lift.T, kernel_1a, kernel_2, kernel_1b, kernel_0b, head, dest)
    mine, *raw = deposit(velocity, cell_list, slot_weight, raw)
    kernel_0a, lifting, kernel_1a, kernel_2, kernel_1b, kernel_0b, head, dest = raw
    theirs = mate(mine)
    near = cross(cat([mine, either(theirs[0:1], theirs[1:2])], 0))
    chip = cat([either(mine, theirs), either(theirs, mine)], 0)

    (w0a,) = in_vmem(first_kernel, [((768, 512), bf16)], (lifting, kernel_0a))
    w1a, w2 = in_vmem(
        middle_kernel,
        [((9, 256, 256), bf16), ((9, 128, 128), bf16)],
        (kernel_1a, kernel_2),
        (theirs,),
    )
    near, w0a, w1a, w2 = barrier(near, w0a, w1a, w2)
    far = mate(near)
    left, right = either(near, far), either(far, near)
    wide = cat([left[2:3], left[0:2], chip, right], 0)
    near = along_y(
        either(
            cat([wide[:, 10:16], wide[:, 26:32]], 1), cat([wide[:, 0:6], wide[:, 16:22]], 1)
        )
    )
    own = either(wide[0:8], wide[2:10])
    fine = own_part(own, w0a, fixed[0])
    w1b, w0b, headed, rank = in_vmem(
        last_kernel,
        [((9, 256, 256), bf16), ((9, 512, 512), bf16), ((512, 128), bf16), ((16, 128), i32)],
        (head, dest, kernel_1b, kernel_0b),
        (own,),
    )
    weights = (w0a, w1a, w2, w1b, w0b)
    near, fine, weights, headed, rank = barrier(near, fine, weights, headed, rank)
    far = mate(either(near[2:10], near[0:8]))
    near = either(near[0:8], near[2:10])
    low, high = either(near, far), either(far, near)

    packed = network(
        own,
        low,
        high,
        fine,
        weights,
        headed,
        fixed,
        position.reshape(3, 16, 128),
        velocity.reshape(3, 16, 128),
        particle_cell.reshape(16, 128),
        dest,
        rank,
    )

    behind, level, ahead = packed[0:72], packed[72:144], packed[144:216]
    from_mate = mate(either(ahead, behind))
    from_cross = cross(either(behind, ahead))
    behind = either(from_mate, from_cross)
    ahead = either(from_cross, from_mate)
    groups = (behind, level, ahead)
    down = cat([group[0:24] for group in groups], 0)
    upward = cat([group[48:72] for group in groups], 0)
    upward, down = along(upward, 1), along(down, -1)
    blocks = []
    for a in range(3):
        blocks.append(down[24 * a : 24 * a + 24])
        blocks.append(groups[a][24:48])
        blocks.append(upward[24 * a : 24 * a + 24])
    inbox = jnp.stack(blocks, axis=0).reshape(9, 6, CAP)
    return inbox.astype(f32).transpose(1, 0, 2).reshape(6, 9 * CAP)


def solution(mesh):
    in_specs = (
        P(None, ("gx", "gy")),
        P(None, ("gx", "gy")),
        P(None, "gx", "gy", None),
        P(None, "gx", "gy", None),
        P(("gx", "gy")),
        P(("gx", "gy"), None),
        P(),
        P(),
        P(),
        P(),
        P(),
        P(),
        P(),
    )
    out_specs = P(None, ("gx", "gy"))
    return jax.shard_map(body, mesh=mesh, in_specs=in_specs, out_specs=out_specs, check_vma=False)
```

```python
import jax
import jax.numpy as jnp
import numpy as np
from jax import lax
from jax.experimental import pallas as pl
from jax.experimental.pallas import tpu as pltpu
from jax.sharding import PartitionSpec as P

f32 = jnp.float32
bf16 = jnp.bfloat16
i32 = jnp.int32

CAP = 512
DRIFT = 0.25
CH = 32
NZ = 16
COLS = 28


def iota(shape, dim):
    return lax.broadcasted_iota(i32, shape, dim)


def dot(a, b):
    return jnp.dot(a, b, preferred_element_type=f32)


def gelu(x):
    inner = x * (0.7978845608028654 + 0.035677408136300125 * (x * x))
    return (0.5 * x) * (1.0 + jnp.tanh(inner))


def pick_lanes(table, lane):
    numbers = lax.GatherDimensionNumbers(
        offset_dims=(),
        collapsed_slice_dims=(1,),
        start_index_map=(1,),
        operand_batching_dims=(0,),
        start_indices_batching_dims=(0,),
    )
    return lax.gather(
        table,
        lane[..., None],
        numbers,
        (1, 1),
        mode=lax.GatherScatterMode.PROMISE_IN_BOUNDS,
    )


def fetch_all(pairs, sems):
    copies = [
        pltpu.make_async_copy(source, target, sems.at[index])
        for index, (source, target) in enumerate(pairs)
    ]
    for copy in copies:
        copy.start()
    return copies


def deposit_kernel(*refs):
    vel_hbm, cells_hbm, weight_hbm = refs[:3]
    raw_in, out_ref, raw_out = refs[3:10], refs[10], refs[11:18]
    stage, vel_ref, cells_ref, weight_ref, sems, raw_sems = refs[18:]
    fetch_vel, fetch_cells, fetch_weight = fetch_all(
        ((vel_hbm, vel_ref), (cells_hbm, cells_ref), (weight_hbm, weight_ref)), sems
    )
    raw_fetches = fetch_all(zip(raw_in, raw_out), raw_sems)

    def dense(ref, s):
        return jnp.concatenate(
            [jnp.concatenate([ref[s, 2 * a + b] for a in range(4)], axis=1) for b in range(2)],
            axis=0,
        )

    fetch_vel.wait()
    fetch_cells.wait()
    entries = [dense(cells_ref, s) for s in range(4)]
    tables = [
        [
            jnp.broadcast_to(vel_ref[q : q + 1, r * 128 : (r + 1) * 128], (8, 128))
            for q in range(3)
        ]
        for r in range(16)
    ]
    picked = []
    for s in range(4):
        pieces = [[], [], []]
        for begin in range(0, 32, 8):
            entry = entries[s][begin : begin + 8]
            lane = jnp.bitwise_and(entry, 127)
            row = jnp.right_shift(entry, 7)
            found = [jnp.zeros((8, 128), f32) for _ in range(3)]
            for r in range(16):
                here = row == r
                for q in range(3):
                    found[q] = jnp.where(here, pick_lanes(tables[r][q], lane), found[q])
            for q in range(3):
                pieces[q].append(found[q])
        picked.append([jnp.concatenate(piece, axis=0) for piece in pieces])
    fetch_weight.wait()
    totals = [jnp.zeros((32, 128), f32) for _ in range(4)]
    for s in range(4):
        weight = dense(weight_ref, s)
        totals[0] = totals[0] + jnp.where(entries[s] < 2048, weight, 0.0)
        for q in range(3):
            totals[q + 1] = totals[q + 1] + weight * picked[s][q]
    stage[...] = jnp.concatenate(
        [totals[q][b * 16 : b * 16 + 16] for b in range(2) for q in range(4)], axis=0
    ).T
    for t in range(4):
        for parity in range(2):
            lanes = slice((t % 2) * 128, (t % 2) * 128 + 128)
            out_ref[t // 2, parity * 16 : parity * 16 + 16, lanes] = stage[
                pl.ds(t * 32 + parity, 16, stride=2), :
            ].astype(bf16)
    for fetch in raw_fetches:
        fetch.wait()


def deposit(velocity, cells, weight, raw):
    return pl.pallas_call(
        deposit_kernel,
        out_shape=(
            pltpu.VMEM((2, 32, 256), bf16),
            *(pltpu.VMEM(value.shape, value.dtype) for value in raw),
        ),
        in_specs=[pl.BlockSpec(memory_space=pltpu.HBM)] * 10,
        out_specs=[pl.BlockSpec(memory_space=pltpu.VMEM)] * 8,
        scratch_shapes=[
            pltpu.VMEM((128, 128), f32),
            pltpu.VMEM((3, 2048), f32),
            pltpu.VMEM((4, 8, 16, 32), i32),
            pltpu.VMEM((4, 8, 16, 32), f32),
            pltpu.SemaphoreType.DMA((3,)),
            pltpu.SemaphoreType.DMA((7,)),
        ],
        cost_estimate=pl.CostEstimate(flops=2_000_000, bytes_accessed=1_000_000, transcendentals=0),
    )(velocity, jnp.swapaxes(cells, 2, 3), jnp.swapaxes(weight, 2, 3), *raw)


def contract_last(a, b):
    return lax.dot_general(a, b, (((1,), (1,)), ((), ())), preferred_element_type=f32)


def first_kernel(lift_ref, kernel_ref, w0a_ref):
    rest = lift_ref[...]
    terms = []
    for _ in range(3):
        term = rest.astype(bf16).astype(f32)
        terms.append(term)
        rest = rest - term
    terms = jnp.concatenate(terms + [jnp.zeros((4, 32), f32)], axis=0).astype(bf16)
    row = iota((16, 128), 0)
    masks = []
    for t in range(4):
        diff = jnp.bitwise_and(row - (4 * t + iota((16, 128), 1) // 32), 15)
        masks.append((diff == 15, diff == 0, diff == 1))
    for ox in range(3):
        for oy in range(3):
            at = 9 * ox + 3 * oy
            repeated = [kernel_ref[at + oz] for oz in range(3) for _ in range(4)]
            parts = contract_last(terms, jnp.concatenate(repeated, axis=0))
            both = parts[0:4] + parts[4:8] + parts[8:12]
            for q in range(4):
                low, mid, high = (
                    jnp.broadcast_to(both[q : q + 1, oz * 128 : oz * 128 + 128], (16, 128))
                    for oz in range(3)
                )
                for t in range(4):
                    below, same, above = masks[t]
                    piece = jnp.where(
                        same, mid, jnp.where(below, low, jnp.where(above, high, 0.0))
                    )
                    begin = oy * 256 + ox * 64 + q * 16
                    w0a_ref[begin : begin + 16, t * 128 : (t + 1) * 128] = piece.astype(bf16)
    for oy in range(3):
        w0a_ref[oy * 256 + 192 : oy * 256 + 256, :] = jnp.zeros((64, 512), bf16)


def bands(kernel_ref, out_ref, depth):
    group = iota((32, 128), 1) // 32
    zero = jnp.zeros((32, 128), f32)
    tiles = depth // 4

    def one(tap, carry):
        row = jnp.concatenate(
            [kernel_ref[3 * tap + oz].astype(f32) for oz in range(3)] + [zero[:, 0:32]], axis=1
        )
        turned = jnp.concatenate([row] * 4, axis=0).T
        low, mid, high = (turned[oz * 32 : oz * 32 + 32] for oz in range(3))

        def pick(*wanted):
            value = zero
            for index, piece in wanted:
                value = jnp.where(group == index, piece, value)
            return value

        patterns = (
            {0: pick((0, mid), (1, low)), -1: pick((3, high))},
            {0: pick((0, high), (1, mid), (2, low))},
            {0: pick((1, high), (2, mid), (3, low))},
            {0: pick((2, high), (3, mid)), 1: pick((0, low))},
        )
        for z in range(depth):
            content = {}
            for step, piece in patterns[z % 4].items():
                tile = (z // 4 + step) % tiles
                content[tile] = content[tile] + piece if tile in content else piece
            for tile in range(tiles):
                out_ref[tap, z * 32 : (z + 1) * 32, tile * 128 : (tile + 1) * 128] = (
                    content.get(tile, zero).astype(bf16)
                )
        return carry

    lax.fori_loop(0, 9, one, 0, unroll=3)


def middle_kernel(k1a_ref, k2_ref, after_ref, w1a_ref, w2_ref):
    bands(k1a_ref, w1a_ref, 8)
    bands(k2_ref, w2_ref, 4)


def last_kernel(
    head_ref, dest_ref, k1b_ref, k0b_ref, after_ref, w1b_ref, w0b_ref, headed_ref, rank_ref
):
    bands(k1b_ref, w1b_ref, 8)
    bands(k0b_ref, w0b_ref, 16)

    row16 = iota((16, 128), 0)
    names = head_ref[...].astype(f32)
    names = jnp.concatenate([names] * 4, axis=1)
    for t in range(4):
        same = row16 == 4 * t + iota((16, 128), 1) // 32
        rows = [
            jnp.where(same, jnp.broadcast_to(names[k : k + 1], (16, 128)), 0.0) for k in range(3)
        ]
        rows.append(jnp.zeros((80, 128), f32))
        headed_ref[t * 128 : t * 128 + 128, :] = jnp.concatenate(rows, axis=0).T.astype(bf16)

    dest = dest_ref[...]
    upper = (iota((128, 128), 0) <= iota((128, 128), 1)).astype(f32).astype(bf16)
    before = (iota((16, 16), 1) < iota((16, 16), 0)).astype(f32).astype(bf16)
    rank = jnp.zeros((16, 128), f32)
    for k in range(9):
        chosen = (dest == k).astype(f32)
        marks = chosen.astype(bf16)
        inside = dot(marks, upper)
        earlier = jnp.sum(dot(before, marks), axis=1, keepdims=True)
        rank = rank + chosen * (inside - 1.0 + earlier)
    rank_ref[...] = rank.astype(i32)


def in_vmem(kernel, shapes, values, after=()):
    vmem = pl.BlockSpec(memory_space=pltpu.VMEM)
    return pl.pallas_call(
        kernel,
        out_shape=tuple(pltpu.VMEM(shape, dtype) for shape, dtype in shapes),
        in_specs=[vmem] * len(values) + [pl.BlockSpec(memory_space=pl.ANY)] * len(after),
        out_specs=(vmem,) * len(shapes),
        compiler_params=pltpu.CompilerParams(vmem_limit_bytes=16 * 2**20),
        cost_estimate=pl.CostEstimate(
            flops=5_000_000, bytes_accessed=5_000_000, transcendentals=0
        ),
    )(*values, *after)


def lanes_of(ref):
    return jnp.concatenate([ref[chunk].astype(f32) for chunk in range(8)], axis=1)


def spread(value, taps_ref, targets):
    plain = value.astype(bf16)
    rolled = pltpu.roll(value, 2048 - 64, 1).astype(bf16)
    for column in range(COLS):
        if column % 2:
            piece = plain[:, 64 * (column + 1) : 64 * (column + 1) + 256]
        else:
            piece = rolled[:, 64 * column : 64 * column + 256]
        for oy, half in targets:
            begin = column * 32 + half * 16
            taps_ref[begin : begin + 16, oy * 256 : oy * 256 + 256] = piece


def first_conv(taps_ref, weight_ref, sums_ref, keep):
    for block in range(COLS // 4):
        value = gelu(dot(taps_ref[block * 128 : block * 128 + 128, :], weight_ref[...])).astype(bf16)
        keep(block, value)
        quads = value.astype(f32).reshape(2, 4, 16, 512)
        summed = (quads[:, 0] + quads[:, 1]) + (quads[:, 2] + quads[:, 3])
        sums_ref[block * 32 : block * 32 + 32, :] = summed.reshape(32, 512).astype(bf16)


def own_kernel(own_ref, w0a_ref, pool_ref, e0_ref, p1_ref, taps, sums):
    own = lanes_of(own_ref)
    even, odd = own[0:16], own[16:32]
    spread(pltpu.roll(odd, 1, 0), taps, ((0, 0),))
    spread(even, taps, ((0, 1), (1, 0)))
    spread(odd, taps, ((1, 1), (2, 0)))
    spread(pltpu.roll(even, 15, 0), taps, ((2, 1),))

    def keep(block, value):
        for column in range(4):
            n = block * 4 + column - 9
            if 0 <= n < 10:
                e0_ref[n * 32 : n * 32 + 32, :] = value[column * 32 : column * 32 + 32]

    first_conv(taps, w0a_ref, sums, keep)
    p1_ref[...] = dot(sums[...], pool_ref[...]).astype(bf16)


def own_part(own, w0a, pool):
    return pl.pallas_call(
        own_kernel,
        out_shape=(pltpu.VMEM((320, 512), bf16), pltpu.VMEM((224, 256), bf16)),
        scratch_shapes=[pltpu.VMEM((COLS * 32, 768), bf16), pltpu.VMEM((224, 512), bf16)],
        compiler_params=pltpu.CompilerParams(vmem_limit_bytes=16 * 2**20),
        cost_estimate=pl.CostEstimate(
            flops=2_000_000_000, bytes_accessed=2_000_000, transcendentals=500_000
        ),
    )(own, w0a, pool)


def network_kernel(
    own_ref,
    low_ref,
    high_ref,
    own_e0_ref,
    own_p1_ref,
    w0a_ref,
    w1a_ref,
    w2_ref,
    w1b_ref,
    w0b_ref,
    head_ref,
    pool_ref,
    grow_ref,
    pool1_ref,
    grow1_ref,
    rowpool_ref,
    rowgrow_ref,
    pos_ref,
    vel_ref,
    where_ref,
    dest_ref,
    rank_ref,
    out_ref,
    even,
    odd,
    taps,
    sums,
    e0_ref,
    p1_ref,
    p2_ref,
    u1_ref,
    ue_ref,
    uo_ref,
    um,
    u0,
    up,
):
    low = lanes_of(low_ref)
    high = lanes_of(high_ref)
    own = lanes_of(own_ref)
    for parity, ref in ((0, even), (1, odd)):
        ref[0:2, :] = jnp.zeros((2, 2048), f32)
        ref[2:8, :] = low[6 * parity : 6 * parity + 6]
        ref[8:24, :] = own[16 * parity : 16 * parity + 16]
        ref[24:30, :] = high[6 * parity : 6 * parity + 6]
        ref[30:32, :] = jnp.zeros((2, 2048), f32)

    def outer(ref, first):
        return jnp.concatenate([ref[first : first + 8, :], ref[first + 22 : first + 30, :]], axis=0)

    spread(outer(odd, 0), taps, ((0, 0),))
    spread(outer(even, 1), taps, ((0, 1), (1, 0)))
    spread(outer(odd, 1), taps, ((1, 1), (2, 0)))
    spread(outer(even, 2), taps, ((2, 1),))

    for n in range(10):
        for parity in range(2):
            at = n * 64 + parity * 32
            begin = n * 32 + parity * 16
            e0_ref[at + 8 : at + 24, :] = own_e0_ref[begin : begin + 16, :].astype(f32)

    def keep(block, value):
        for column in range(4):
            n = block * 4 + column - 9
            if 0 <= n < 10:
                for parity in range(2):
                    at = n * 64 + parity * 32
                    begin = column * 32 + parity * 16
                    rows = value[begin : begin + 16].astype(f32)
                    e0_ref[at + 1 : at + 9, :] = rows[0:8]
                    e0_ref[at + 23 : at + 31, :] = rows[8:16]

    first_conv(taps, w0a_ref, sums, keep)
    pooled = dot(sums[...], pool_ref[...]).astype(bf16).astype(f32)
    own_pooled = own_p1_ref[...].astype(f32)
    p1_ref[...] = jnp.zeros((464, 256), f32)
    for column in range(14):
        at = 8 + column * 32
        p1_ref[at + 8 : at + 24, :] = own_pooled[column * 16 : column * 16 + 16]
        p1_ref[at + 1 : at + 9, :] = pooled[column * 16 : column * 16 + 8]
        p1_ref[at + 23 : at + 31, :] = pooled[column * 16 + 8 : column * 16 + 16]

    def middle(ref, blocks, weight_ref, stride, size, pad):
        shifted = [ref[pad + oy - 1 : pad + oy - 1 + size, :].astype(bf16) for oy in range(3)]
        pieces = [
            shifted[oy][ox * stride : ox * stride + blocks * stride]
            for ox in range(3)
            for oy in range(3)
        ]
        width = weight_ref.shape[2]
        total = dot(jnp.concatenate(pieces, axis=1), weight_ref[...].reshape(9 * width, width))
        return gelu(total).astype(bf16)

    e1 = middle(p1_ref, 12, w1a_ref, 32, 448, 8)
    part = dot(rowpool_ref[...], e1).astype(bf16)
    p2_ref[0:8, :] = jnp.zeros((8, 128), f32)
    p2_ref[104:112, :] = jnp.zeros((8, 128), f32)
    p2_ref[8:104, :] = dot(part, pool1_ref[...]).astype(bf16).astype(f32)
    e2 = middle(p2_ref, 4, w2_ref, 16, 96, 8)
    grown = dot(dot(rowgrow_ref[...], e2).astype(bf16), grow1_ref[...])
    u1_ref[0:8, :] = jnp.zeros((8, 256), f32)
    u1_ref[264:272, :] = jnp.zeros((8, 256), f32)
    u1_ref[8:264, :] = (e1[64:320].astype(f32) + grown).astype(bf16).astype(f32)
    f1 = middle(u1_ref, 6, w1b_ref, 32, 256, 8)
    grown = dot(f1, grow_ref[...])
    for n in range(10):
        add = grown[((n + 1) // 2) * 32 : ((n + 1) // 2) * 32 + 32]
        begin = n * 64
        ue_ref[...] = (e0_ref[begin : begin + 32, :] + add).astype(bf16).astype(f32)
        uo_ref[...] = (e0_ref[begin + 32 : begin + 64, :] + add).astype(bf16).astype(f32)
        at = n * 32
        even_here = ue_ref[8:24, :].astype(bf16)
        odd_here = uo_ref[8:24, :].astype(bf16)
        um[at : at + 16, :] = uo_ref[7:23, :].astype(bf16)
        um[at + 16 : at + 32, :] = even_here
        u0[at : at + 16, :] = even_here
        u0[at + 16 : at + 32, :] = odd_here
        up[at : at + 16, :] = odd_here
        up[at + 16 : at + 32, :] = ue_ref[9:25, :].astype(bf16)

    pieces = [ref[ox * 32 : ox * 32 + 256, :] for ox in range(3) for ref in (um, u0, up)]
    total = dot(jnp.concatenate(pieces, axis=1), w0b_ref[...].reshape(9 * 512, 512))
    change = dot(gelu(total).astype(bf16), head_ref[...])

    lane16 = iota((32, 128), 1) // 16
    tables = []
    for comp in range(3):
        table = jnp.zeros((32, 128), f32)
        for x in range(8):
            block = change[x * 32 : x * 32 + 32]
            shift = ((x - comp) * 16) % 128
            moved = pltpu.roll(block, shift, 1) if shift else block
            table = jnp.where(lane16 == x, moved, table)
        tables.append(table)
    cell = where_ref[...]
    y = jnp.bitwise_and(jnp.right_shift(cell, 4), 31)
    row = jnp.bitwise_and(y, 1) * 16 + jnp.right_shift(y, 1)
    lane = jnp.right_shift(cell, 9) * 16 + jnp.bitwise_and(cell, 15)
    pieces = [[], [], []]
    for begin in (0, 8):
        row_here, lane_here = row[begin : begin + 8], lane[begin : begin + 8]
        found = [jnp.zeros((8, 128), f32) for _ in range(3)]
        for r in range(32):
            here = row_here == r
            for comp in range(3):
                source = jnp.broadcast_to(tables[comp][r : r + 1], (8, 128))
                found[comp] = jnp.where(here, pick_lanes(source, lane_here), found[comp])
        for comp in range(3):
            pieces[comp].append(found[comp])
    kick = [jnp.concatenate(piece, axis=0) for piece in pieces]
    payload = []
    speeds = [vel_ref[comp] + kick[comp] for comp in range(3)]
    for comp in range(3):
        payload.append(pos_ref[comp] + DRIFT * speeds[comp])
    payload = payload + speeds

    rank = rank_ref[...]
    key = dest_ref[...] * 4 + jnp.right_shift(rank, 7)
    slot = jnp.bitwise_and(rank, 127)
    line = iota((216, 128), 0)
    line_key = (line // 24) * 4 + jnp.bitwise_and(line, 3)
    slots = iota((128, 128), 0)
    packed = jnp.zeros((216, 128), f32)
    for pair in range(8):
        left, right = [], []
        for c in (2 * pair, 2 * pair + 1):
            rows = jnp.concatenate(
                [jnp.broadcast_to(part[c : c + 1], (4, 128)) for part in payload], axis=0
            )
            full = jnp.concatenate([rows] * 9, axis=0)
            left.append(jnp.where(line_key == key[c : c + 1], full, 0.0).astype(bf16))
            right.append((slots == slot[c : c + 1]).astype(f32).astype(bf16))
        packed = packed + contract_last(
            jnp.concatenate(left, axis=1), jnp.concatenate(right, axis=1)
        )
    out_ref[...] = packed.astype(bf16)


def constants():
    pool = np.zeros((NZ * CH, NZ // 2 * CH), np.float32)
    for z in range(NZ):
        for c in range(CH):
            pool[z * CH + c, z // 2 * CH + c] = 1.0
    pool1 = pool[: 8 * CH, : 4 * CH]
    rowpool = np.zeros((96, 384), np.float32)
    for a in range(6):
        for s in range(12):
            for dx in range(2):
                for dy in range(2):
                    rowpool[a * 16 + s, (2 * a + dx) * 32 + 2 * s + 4 + dy] = 0.25
    rowgrow = np.zeros((256, 64), np.float32)
    for c in range(8):
        for r in range(6, 26):
            rowgrow[c * 32 + r, (c // 2) * 16 + (r - 4) // 2] = 1.0
    made = (pool * 0.125, pool.T, pool1 * 0.5, pool1.T, rowpool, rowgrow)
    return [jnp.asarray(np.ascontiguousarray(value), bf16) for value in made]


def network(own, low, high, fine, weights, head, fixed, pos, vel, where, dest, rank):
    vmem = pl.BlockSpec(memory_space=pltpu.VMEM)
    return pl.pallas_call(
        network_kernel,
        out_shape=pltpu.VMEM((216, 128), bf16),
        in_specs=[vmem] * 22,
        out_specs=vmem,
        scratch_shapes=[
            pltpu.VMEM((32, 2048), f32),
            pltpu.VMEM((32, 2048), f32),
            pltpu.VMEM((COLS * 32, 768), bf16),
            pltpu.VMEM((224, 512), bf16),
            pltpu.VMEM((640, 512), f32),
            pltpu.VMEM((464, 256), f32),
            pltpu.VMEM((112, 128), f32),
            pltpu.VMEM((272, 256), f32),
            pltpu.VMEM((32, 512), f32),
            pltpu.VMEM((32, 512), f32),
            pltpu.VMEM((320, 512), bf16),
            pltpu.VMEM((320, 512), bf16),
            pltpu.VMEM((320, 512), bf16),
        ],
        compiler_params=pltpu.CompilerParams(vmem_limit_bytes=36 * 2**20),
        cost_estimate=pl.CostEstimate(
            flops=3_000_000_000, bytes_accessed=10_000_000, transcendentals=1_000_000
        ),
    )(own, low, high, *fine, *weights, head, *fixed, pos, vel, where, dest, rank)


def exchange(value, count_x, count_y, rule):
    pairs = []
    for i in range(count_x):
        for j in range(count_y):
            a, b = rule(i, j)
            pairs.append((i * count_y + j, (a % count_x) * count_y + b % count_y))
    return lax.ppermute(value, ("gx", "gy"), pairs)


def body(
    position,
    velocity,
    cell_list,
    slot_weight,
    particle_cell,
    destination,
    lift,
    kernel_0a,
    kernel_1a,
    kernel_2,
    kernel_1b,
    kernel_0b,
    head,
):
    count_x, count_y = lax.axis_size("gx"), lax.axis_size("gy")
    first_core = lax.rem(lax.axis_index("gx"), 2) == 0

    def mate(value):
        return exchange(value, count_x, count_y, lambda i, j: (i ^ 1, j))

    def cross(value):
        return exchange(value, count_x, count_y, lambda i, j: (i + 1 if i % 2 else i - 1, j))

    def along_y(value):
        return exchange(value, count_x, count_y, lambda i, j: (i, j - 1 if i % 2 else j + 1))

    def along(value, step):
        return exchange(value, count_x, count_y, lambda i, j: (i, j + step))

    def either(if_first, if_second):
        return jnp.where(first_core, if_first, if_second)

    def cat(parts, axis):
        return jnp.concatenate(parts, axis=axis)

    def barrier(*values):
        return lax.optimization_barrier(values)

    fixed = constants()
    dest = destination.reshape(16, 128)

    raw = (kernel_0a, lift.T, kernel_1a, kernel_2, kernel_1b, kernel_0b, dest)
    mine, *raw = deposit(velocity, cell_list, slot_weight, raw)
    kernel_0a, lifting, kernel_1a, kernel_2, kernel_1b, kernel_0b, dest = raw
    theirs = mate(mine)
    near = cross(cat([mine, either(theirs[0:1], theirs[1:2])], 0))
    chip = cat([either(mine, theirs), either(theirs, mine)], 0)

    (w0a,) = in_vmem(first_kernel, [((768, 512), bf16)], (lifting, kernel_0a))
    w1a, w2 = in_vmem(
        middle_kernel,
        [((9, 256, 256), bf16), ((9, 128, 128), bf16)],
        (kernel_1a, kernel_2),
        (theirs,),
    )
    near, w0a, w1a, w2 = barrier(near, w0a, w1a, w2)
    far = mate(near)
    left, right = either(near, far), either(far, near)
    wide = cat([left[2:3], left[0:2], chip, right], 0)
    near = along_y(
        either(
            cat([wide[:, 10:16], wide[:, 26:32]], 1), cat([wide[:, 0:6], wide[:, 16:22]], 1)
        )
    )
    own = either(wide[0:8], wide[2:10])
    fine = own_part(own, w0a, fixed[0])
    w1b, w0b, headed, rank = in_vmem(
        last_kernel,
        [((9, 256, 256), bf16), ((9, 512, 512), bf16), ((512, 128), bf16), ((16, 128), i32)],
        (head, dest, kernel_1b, kernel_0b),
        (own,),
    )
    weights = (w0a, w1a, w2, w1b, w0b)
    near, fine, weights, headed, rank = barrier(near, fine, weights, headed, rank)
    far = mate(either(near[2:10], near[0:8]))
    near = either(near[0:8], near[2:10])
    low, high = either(near, far), either(far, near)

    packed = network(
        own,
        low,
        high,
        fine,
        weights,
        headed,
        fixed,
        position.reshape(3, 16, 128),
        velocity.reshape(3, 16, 128),
        particle_cell.reshape(16, 128),
        dest,
        rank,
    )

    behind, level, ahead = packed[0:72], packed[72:144], packed[144:216]
    from_mate = mate(either(ahead, behind))
    from_cross = cross(either(behind, ahead))
    behind = either(from_mate, from_cross)
    ahead = either(from_cross, from_mate)
    groups = (behind, level, ahead)
    down = cat([group[0:24] for group in groups], 0)
    upward = cat([group[48:72] for group in groups], 0)
    upward, down = along(upward, 1), along(down, -1)
    blocks = []
    for a in range(3):
        blocks.append(down[24 * a : 24 * a + 24])
        blocks.append(groups[a][24:48])
        blocks.append(upward[24 * a : 24 * a + 24])
    inbox = jnp.stack(blocks, axis=0).reshape(9, 6, CAP)
    return inbox.astype(f32).transpose(1, 0, 2).reshape(6, 9 * CAP)


def solution(mesh):
    in_specs = (
        P(None, ("gx", "gy")),
        P(None, ("gx", "gy")),
        P(None, "gx", "gy", None),
        P(None, "gx", "gy", None),
        P(("gx", "gy")),
        P(("gx", "gy"), None),
        P(),
        P(),
        P(),
        P(),
        P(),
        P(),
        P(),
    )
    out_specs = P(None, ("gx", "gy"))
    return jax.shard_map(body, mesh=mesh, in_specs=in_specs, out_specs=out_specs, check_vma=False)
```

```python
import jax
import jax.numpy as jnp
import numpy as np
from jax import lax
from jax.experimental import pallas as pl
from jax.experimental.pallas import tpu as pltpu
from jax.sharding import PartitionSpec as P

f32 = jnp.float32
bf16 = jnp.bfloat16
i32 = jnp.int32

CAP = 512
DRIFT = 0.25
CH = 32
NZ = 16
COLS = 28


def iota(shape, dim):
    return lax.broadcasted_iota(i32, shape, dim)


def dot(a, b):
    return jnp.dot(a, b, preferred_element_type=f32)


def gelu(x):
    inner = x * (0.7978845608028654 + 0.035677408136300125 * (x * x))
    return (0.5 * x) * (1.0 + jnp.tanh(inner))


def pick_lanes(table, lane):
    numbers = lax.GatherDimensionNumbers(
        offset_dims=(),
        collapsed_slice_dims=(1,),
        start_index_map=(1,),
        operand_batching_dims=(0,),
        start_indices_batching_dims=(0,),
    )
    return lax.gather(
        table,
        lane[..., None],
        numbers,
        (1, 1),
        mode=lax.GatherScatterMode.PROMISE_IN_BOUNDS,
    )


def fetch_all(pairs, sems):
    copies = [
        pltpu.make_async_copy(source, target, sems.at[index])
        for index, (source, target) in enumerate(pairs)
    ]
    for copy in copies:
        copy.start()
    return copies


def deposit_kernel(*refs):
    vel_hbm, cells_hbm, weight_hbm = refs[:3]
    raw_in, out_ref, raw_out = refs[3:10], refs[10], refs[11:18]
    stage, vel_ref, cells_ref, weight_ref, sems, raw_sems = refs[18:]
    fetch_vel, fetch_cells, fetch_weight = fetch_all(
        ((vel_hbm, vel_ref), (cells_hbm, cells_ref), (weight_hbm, weight_ref)), sems
    )
    raw_fetches = fetch_all(zip(raw_in, raw_out), raw_sems)

    def dense(ref, s):
        return jnp.concatenate(
            [jnp.concatenate([ref[s, 2 * a + b] for a in range(4)], axis=1) for b in range(2)],
            axis=0,
        )

    fetch_vel.wait()
    fetch_cells.wait()
    entries = [dense(cells_ref, s) for s in range(4)]
    tables = [
        [
            jnp.broadcast_to(vel_ref[q : q + 1, r * 128 : (r + 1) * 128], (8, 128))
            for q in range(3)
        ]
        for r in range(16)
    ]
    picked = []
    for s in range(4):
        pieces = [[], [], []]
        for begin in range(0, 32, 8):
            entry = entries[s][begin : begin + 8]
            lane = jnp.bitwise_and(entry, 127)
            row = jnp.right_shift(entry, 7)
            found = [jnp.zeros((8, 128), f32) for _ in range(3)]
            for r in range(16):
                here = row == r
                for q in range(3):
                    found[q] = jnp.where(here, pick_lanes(tables[r][q], lane), found[q])
            for q in range(3):
                pieces[q].append(found[q])
        picked.append([jnp.concatenate(piece, axis=0) for piece in pieces])
    fetch_weight.wait()
    totals = [jnp.zeros((32, 128), f32) for _ in range(4)]
    for s in range(4):
        weight = dense(weight_ref, s)
        totals[0] = totals[0] + jnp.where(entries[s] < 2048, weight, 0.0)
        for q in range(3):
            totals[q + 1] = totals[q + 1] + weight * picked[s][q]
    stage[...] = jnp.concatenate(
        [totals[q][b * 16 : b * 16 + 16] for b in range(2) for q in range(4)], axis=0
    ).T
    for t in range(4):
        for parity in range(2):
            lanes = slice((t % 2) * 128, (t % 2) * 128 + 128)
            out_ref[t // 2, parity * 16 : parity * 16 + 16, lanes] = stage[
                pl.ds(t * 32 + parity, 16, stride=2), :
            ].astype(bf16)
    for fetch in raw_fetches:
        fetch.wait()


def deposit(velocity, cells, weight, raw):
    return pl.pallas_call(
        deposit_kernel,
        out_shape=(
            pltpu.VMEM((2, 32, 256), bf16),
            *(pltpu.VMEM(value.shape, value.dtype) for value in raw),
        ),
        in_specs=[pl.BlockSpec(memory_space=pltpu.HBM)] * 10,
        out_specs=[pl.BlockSpec(memory_space=pltpu.VMEM)] * 8,
        scratch_shapes=[
            pltpu.VMEM((128, 128), f32),
            pltpu.VMEM((3, 2048), f32),
            pltpu.VMEM((4, 8, 16, 32), i32),
            pltpu.VMEM((4, 8, 16, 32), f32),
            pltpu.SemaphoreType.DMA((3,)),
            pltpu.SemaphoreType.DMA((7,)),
        ],
        cost_estimate=pl.CostEstimate(flops=2_000_000, bytes_accessed=1_000_000, transcendentals=0),
    )(velocity, jnp.swapaxes(cells, 2, 3), jnp.swapaxes(weight, 2, 3), *raw)


def contract_last(a, b):
    return lax.dot_general(a, b, (((1,), (1,)), ((), ())), preferred_element_type=f32)


def first_kernel(lift_ref, kernel_ref, w0a_ref):
    rest = lift_ref[...]
    terms = []
    for _ in range(3):
        term = rest.astype(bf16).astype(f32)
        terms.append(term)
        rest = rest - term
    terms = jnp.concatenate(terms + [jnp.zeros((4, 32), f32)], axis=0).astype(bf16)
    row = iota((16, 128), 0)
    masks = []
    for t in range(4):
        diff = jnp.bitwise_and(row - (4 * t + iota((16, 128), 1) // 32), 15)
        masks.append((diff == 15, diff == 0, diff == 1))
    for ox in range(3):
        for oy in range(3):
            at = 9 * ox + 3 * oy
            repeated = [kernel_ref[at + oz] for oz in range(3) for _ in range(4)]
            parts = contract_last(terms, jnp.concatenate(repeated, axis=0))
            both = parts[0:4] + parts[4:8] + parts[8:12]
            for q in range(4):
                low, mid, high = (
                    jnp.broadcast_to(both[q : q + 1, oz * 128 : oz * 128 + 128], (16, 128))
                    for oz in range(3)
                )
                for t in range(4):
                    below, same, above = masks[t]
                    piece = jnp.where(
                        same, mid, jnp.where(below, low, jnp.where(above, high, 0.0))
                    )
                    begin = oy * 256 + ox * 64 + q * 16
                    w0a_ref[begin : begin + 16, t * 128 : (t + 1) * 128] = piece.astype(bf16)
    for oy in range(3):
        w0a_ref[oy * 256 + 192 : oy * 256 + 256, :] = jnp.zeros((64, 512), bf16)


def bands(kernel_ref, out_ref, depth):
    group = iota((32, 128), 1) // 32
    zero = jnp.zeros((32, 128), f32)
    tiles = depth // 4

    def one(tap, carry):
        row = jnp.concatenate(
            [kernel_ref[3 * tap + oz].astype(f32) for oz in range(3)] + [zero[:, 0:32]], axis=1
        )
        turned = jnp.concatenate([row] * 4, axis=0).T
        low, mid, high = (turned[oz * 32 : oz * 32 + 32] for oz in range(3))

        def pick(*wanted):
            value = zero
            for index, piece in wanted:
                value = jnp.where(group == index, piece, value)
            return value

        patterns = (
            {0: pick((0, mid), (1, low)), -1: pick((3, high))},
            {0: pick((0, high), (1, mid), (2, low))},
            {0: pick((1, high), (2, mid), (3, low))},
            {0: pick((2, high), (3, mid)), 1: pick((0, low))},
        )
        for z in range(depth):
            content = {}
            for step, piece in patterns[z % 4].items():
                tile = (z // 4 + step) % tiles
                content[tile] = content[tile] + piece if tile in content else piece
            for tile in range(tiles):
                out_ref[tap, z * 32 : (z + 1) * 32, tile * 128 : (tile + 1) * 128] = (
                    content.get(tile, zero).astype(bf16)
                )
        return carry

    lax.fori_loop(0, 9, one, 0, unroll=3)


def middle_kernel(k1a_ref, k2_ref, after_ref, w1a_ref, w2_ref):
    bands(k1a_ref, w1a_ref, 8)
    bands(k2_ref, w2_ref, 4)


def last_kernel(
    head_ref, dest_ref, k1b_ref, k0b_ref, after_ref, w1b_ref, w0b_ref, headed_ref, rank_ref
):
    bands(k1b_ref, w1b_ref, 8)
    bands(k0b_ref, w0b_ref, 16)

    row16 = iota((16, 128), 0)
    names = head_ref[...].astype(f32)
    names = jnp.concatenate([names] * 4, axis=1)
    for t in range(4):
        same = row16 == 4 * t + iota((16, 128), 1) // 32
        rows = [
            jnp.where(same, jnp.broadcast_to(names[k : k + 1], (16, 128)), 0.0) for k in range(3)
        ]
        rows.append(jnp.zeros((80, 128), f32))
        headed_ref[t * 128 : t * 128 + 128, :] = jnp.concatenate(rows, axis=0).T.astype(bf16)

    dest = dest_ref[...]
    upper = (iota((128, 128), 0) <= iota((128, 128), 1)).astype(f32).astype(bf16)
    before = (iota((16, 16), 1) < iota((16, 16), 0)).astype(f32).astype(bf16)
    rank = jnp.zeros((16, 128), f32)
    for k in range(9):
        chosen = (dest == k).astype(f32)
        marks = chosen.astype(bf16)
        inside = dot(marks, upper)
        earlier = jnp.sum(dot(before, marks), axis=1, keepdims=True)
        rank = rank + chosen * (inside - 1.0 + earlier)
    rank_ref[...] = rank.astype(i32)


def in_vmem(kernel, shapes, values, after=()):
    vmem = pl.BlockSpec(memory_space=pltpu.VMEM)
    return pl.pallas_call(
        kernel,
        out_shape=tuple(pltpu.VMEM(shape, dtype) for shape, dtype in shapes),
        in_specs=[vmem] * len(values) + [pl.BlockSpec(memory_space=pl.ANY)] * len(after),
        out_specs=(vmem,) * len(shapes),
        compiler_params=pltpu.CompilerParams(vmem_limit_bytes=16 * 2**20),
        cost_estimate=pl.CostEstimate(
            flops=5_000_000, bytes_accessed=5_000_000, transcendentals=0
        ),
    )(*values, *after)


def lanes_of(ref):
    return jnp.concatenate([ref[chunk].astype(f32) for chunk in range(8)], axis=1)


def spread(value, taps_ref, targets):
    plain = value.astype(bf16)
    rolled = pltpu.roll(value, 2048 - 64, 1).astype(bf16)
    for column in range(COLS):
        if column % 2:
            piece = plain[:, 64 * (column + 1) : 64 * (column + 1) + 256]
        else:
            piece = rolled[:, 64 * column : 64 * column + 256]
        for oy, half in targets:
            begin = column * 32 + half * 16
            taps_ref[begin : begin + 16, oy * 256 : oy * 256 + 256] = piece


def first_conv(taps_ref, weight_ref, sums_ref, keep):
    for block in range(COLS // 4):
        value = gelu(dot(taps_ref[block * 128 : block * 128 + 128, :], weight_ref[...])).astype(bf16)
        keep(block, value)
        quads = value.astype(f32).reshape(2, 4, 16, 512)
        summed = (quads[:, 0] + quads[:, 1]) + (quads[:, 2] + quads[:, 3])
        sums_ref[block * 32 : block * 32 + 32, :] = summed.reshape(32, 512).astype(bf16)


def own_kernel(own_ref, w0a_ref, pool_ref, e0_ref, p1_ref, taps, sums):
    own = lanes_of(own_ref)
    even, odd = own[0:16], own[16:32]
    spread(pltpu.roll(odd, 1, 0), taps, ((0, 0),))
    spread(even, taps, ((0, 1), (1, 0)))
    spread(odd, taps, ((1, 1), (2, 0)))
    spread(pltpu.roll(even, 15, 0), taps, ((2, 1),))

    def keep(block, value):
        for column in range(4):
            n = block * 4 + column - 9
            if 0 <= n < 10:
                e0_ref[n * 32 : n * 32 + 32, :] = value[column * 32 : column * 32 + 32]

    first_conv(taps, w0a_ref, sums, keep)
    p1_ref[...] = dot(sums[...], pool_ref[...]).astype(bf16)


def own_part(own, w0a, pool):
    return pl.pallas_call(
        own_kernel,
        out_shape=(pltpu.VMEM((320, 512), bf16), pltpu.VMEM((224, 256), bf16)),
        scratch_shapes=[pltpu.VMEM((COLS * 32, 768), bf16), pltpu.VMEM((224, 512), bf16)],
        compiler_params=pltpu.CompilerParams(vmem_limit_bytes=16 * 2**20),
        cost_estimate=pl.CostEstimate(
            flops=2_000_000_000, bytes_accessed=2_000_000, transcendentals=500_000
        ),
    )(own, w0a, pool)


def network_kernel(
    own_ref,
    low_ref,
    high_ref,
    own_e0_ref,
    own_p1_ref,
    w0a_ref,
    w1a_ref,
    w2_ref,
    w1b_ref,
    w0b_ref,
    head_ref,
    pool_ref,
    grow_ref,
    pool1_ref,
    grow1_ref,
    rowpool_ref,
    rowgrow_ref,
    pos_ref,
    vel_ref,
    where_ref,
    dest_ref,
    rank_ref,
    out_ref,
    even,
    odd,
    taps,
    sums,
    e0_ref,
    p1_ref,
    p2_ref,
    u1_ref,
    ue_ref,
    uo_ref,
    um,
    u0,
    up,
):
    low = lanes_of(low_ref)
    high = lanes_of(high_ref)
    own = lanes_of(own_ref)
    for parity, ref in ((0, even), (1, odd)):
        ref[0:2, :] = jnp.zeros((2, 2048), f32)
        ref[2:8, :] = low[6 * parity : 6 * parity + 6]
        ref[8:24, :] = own[16 * parity : 16 * parity + 16]
        ref[24:30, :] = high[6 * parity : 6 * parity + 6]
        ref[30:32, :] = jnp.zeros((2, 2048), f32)

    def outer(ref, first):
        return jnp.concatenate([ref[first : first + 8, :], ref[first + 22 : first + 30, :]], axis=0)

    spread(outer(odd, 0), taps, ((0, 0),))
    spread(outer(even, 1), taps, ((0, 1), (1, 0)))
    spread(outer(odd, 1), taps, ((1, 1), (2, 0)))
    spread(outer(even, 2), taps, ((2, 1),))

    for n in range(10):
        for parity in range(2):
            at = n * 64 + parity * 32
            begin = n * 32 + parity * 16
            e0_ref[at + 8 : at + 24, :] = own_e0_ref[begin : begin + 16, :].astype(f32)

    def keep(block, value):
        for column in range(4):
            n = block * 4 + column - 9
            if 0 <= n < 10:
                for parity in range(2):
                    at = n * 64 + parity * 32
                    begin = column * 32 + parity * 16
                    rows = value[begin : begin + 16].astype(f32)
                    e0_ref[at + 1 : at + 9, :] = rows[0:8]
                    e0_ref[at + 23 : at + 31, :] = rows[8:16]

    first_conv(taps, w0a_ref, sums, keep)
    pooled = dot(sums[...], pool_ref[...]).astype(bf16).astype(f32)
    own_pooled = own_p1_ref[...].astype(f32)
    p1_ref[...] = jnp.zeros((464, 256), f32)
    for column in range(14):
        at = 8 + column * 32
        p1_ref[at + 8 : at + 24, :] = own_pooled[column * 16 : column * 16 + 16]
        p1_ref[at + 1 : at + 9, :] = pooled[column * 16 : column * 16 + 8]
        p1_ref[at + 23 : at + 31, :] = pooled[column * 16 + 8 : column * 16 + 16]

    def middle(ref, blocks, weight_ref, stride, size, pad):
        shifted = [ref[pad + oy - 1 : pad + oy - 1 + size, :].astype(bf16) for oy in range(3)]
        pieces = [
            shifted[oy][ox * stride : ox * stride + blocks * stride]
            for ox in range(3)
            for oy in range(3)
        ]
        width = weight_ref.shape[2]
        total = dot(jnp.concatenate(pieces, axis=1), weight_ref[...].reshape(9 * width, width))
        return gelu(total).astype(bf16)

    e1 = middle(p1_ref, 12, w1a_ref, 32, 448, 8)
    part = dot(rowpool_ref[...], e1).astype(bf16)
    p2_ref[0:8, :] = jnp.zeros((8, 128), f32)
    p2_ref[104:112, :] = jnp.zeros((8, 128), f32)
    p2_ref[8:104, :] = dot(part, pool1_ref[...]).astype(bf16).astype(f32)
    e2 = middle(p2_ref, 4, w2_ref, 16, 96, 8)
    grown = dot(dot(rowgrow_ref[...], e2).astype(bf16), grow1_ref[...])
    u1_ref[0:8, :] = jnp.zeros((8, 256), f32)
    u1_ref[264:272, :] = jnp.zeros((8, 256), f32)
    u1_ref[8:264, :] = (e1[64:320].astype(f32) + grown).astype(bf16).astype(f32)
    f1 = middle(u1_ref, 6, w1b_ref, 32, 256, 8)
    grown = dot(f1, grow_ref[...])
    for n in range(10):
        add = grown[((n + 1) // 2) * 32 : ((n + 1) // 2) * 32 + 32]
        begin = n * 64
        ue_ref[...] = (e0_ref[begin : begin + 32, :] + add).astype(bf16).astype(f32)
        uo_ref[...] = (e0_ref[begin + 32 : begin + 64, :] + add).astype(bf16).astype(f32)
        at = n * 32
        even_here = ue_ref[8:24, :].astype(bf16)
        odd_here = uo_ref[8:24, :].astype(bf16)
        um[at : at + 16, :] = uo_ref[7:23, :].astype(bf16)
        um[at + 16 : at + 32, :] = even_here
        u0[at : at + 16, :] = even_here
        u0[at + 16 : at + 32, :] = odd_here
        up[at : at + 16, :] = odd_here
        up[at + 16 : at + 32, :] = ue_ref[9:25, :].astype(bf16)

    pieces = [ref[ox * 32 : ox * 32 + 256, :] for ox in range(3) for ref in (um, u0, up)]
    total = dot(jnp.concatenate(pieces, axis=1), w0b_ref[...].reshape(9 * 512, 512))
    change = dot(gelu(total).astype(bf16), head_ref[...])

    lane16 = iota((32, 128), 1) // 16
    tables = []
    for comp in range(3):
        table = jnp.zeros((32, 128), f32)
        for x in range(8):
            block = change[x * 32 : x * 32 + 32]
            shift = ((x - comp) * 16) % 128
            moved = pltpu.roll(block, shift, 1) if shift else block
            table = jnp.where(lane16 == x, moved, table)
        tables.append(table)
    cell = where_ref[...]
    y = jnp.bitwise_and(jnp.right_shift(cell, 4), 31)
    row = jnp.bitwise_and(y, 1) * 16 + jnp.right_shift(y, 1)
    lane = jnp.right_shift(cell, 9) * 16 + jnp.bitwise_and(cell, 15)
    pieces = [[], [], []]
    for begin in (0, 8):
        row_here, lane_here = row[begin : begin + 8], lane[begin : begin + 8]
        found = [jnp.zeros((8, 128), f32) for _ in range(3)]
        for r in range(32):
            here = row_here == r
            for comp in range(3):
                source = jnp.broadcast_to(tables[comp][r : r + 1], (8, 128))
                found[comp] = jnp.where(here, pick_lanes(source, lane_here), found[comp])
        for comp in range(3):
            pieces[comp].append(found[comp])
    kick = [jnp.concatenate(piece, axis=0) for piece in pieces]
    payload = []
    speeds = [vel_ref[comp] + kick[comp] for comp in range(3)]
    for comp in range(3):
        payload.append(pos_ref[comp] + DRIFT * speeds[comp])
    payload = payload + speeds

    rank = rank_ref[...]
    key = dest_ref[...] * 4 + jnp.right_shift(rank, 7)
    slot = jnp.bitwise_and(rank, 127)
    line = iota((216, 128), 0)
    line_key = (line // 24) * 4 + jnp.bitwise_and(line, 3)
    slots = iota((128, 128), 0)
    packed = jnp.zeros((216, 128), f32)
    for pair in range(8):
        left, right = [], []
        for c in (2 * pair, 2 * pair + 1):
            rows = jnp.concatenate(
                [jnp.broadcast_to(part[c : c + 1], (4, 128)) for part in payload], axis=0
            )
            full = jnp.concatenate([rows] * 9, axis=0)
            left.append(jnp.where(line_key == key[c : c + 1], full, 0.0).astype(bf16))
            right.append((slots == slot[c : c + 1]).astype(f32).astype(bf16))
        packed = packed + contract_last(
            jnp.concatenate(left, axis=1), jnp.concatenate(right, axis=1)
        )
    out_ref[...] = packed.astype(bf16)


def constants():
    pool = np.zeros((NZ * CH, NZ // 2 * CH), np.float32)
    for z in range(NZ):
        for c in range(CH):
            pool[z * CH + c, z // 2 * CH + c] = 1.0
    pool1 = pool[: 8 * CH, : 4 * CH]
    rowpool = np.zeros((96, 384), np.float32)
    for a in range(6):
        for s in range(12):
            for dx in range(2):
                for dy in range(2):
                    rowpool[a * 16 + s, (2 * a + dx) * 32 + 2 * s + 4 + dy] = 0.25
    rowgrow = np.zeros((256, 64), np.float32)
    for c in range(8):
        for r in range(6, 26):
            rowgrow[c * 32 + r, (c // 2) * 16 + (r - 4) // 2] = 1.0
    made = (pool * 0.125, pool.T, pool1 * 0.5, pool1.T, rowpool, rowgrow)
    return [jnp.asarray(np.ascontiguousarray(value), bf16) for value in made]


def network(own, low, high, fine, weights, head, fixed, pos, vel, where, dest, rank):
    vmem = pl.BlockSpec(memory_space=pltpu.VMEM)
    return pl.pallas_call(
        network_kernel,
        out_shape=pltpu.VMEM((216, 128), bf16),
        in_specs=[vmem] * 22,
        out_specs=vmem,
        scratch_shapes=[
            pltpu.VMEM((32, 2048), f32),
            pltpu.VMEM((32, 2048), f32),
            pltpu.VMEM((COLS * 32, 768), bf16),
            pltpu.VMEM((224, 512), bf16),
            pltpu.VMEM((640, 512), f32),
            pltpu.VMEM((464, 256), f32),
            pltpu.VMEM((112, 128), f32),
            pltpu.VMEM((272, 256), f32),
            pltpu.VMEM((32, 512), f32),
            pltpu.VMEM((32, 512), f32),
            pltpu.VMEM((320, 512), bf16),
            pltpu.VMEM((320, 512), bf16),
            pltpu.VMEM((320, 512), bf16),
        ],
        compiler_params=pltpu.CompilerParams(vmem_limit_bytes=36 * 2**20),
        cost_estimate=pl.CostEstimate(
            flops=3_000_000_000, bytes_accessed=10_000_000, transcendentals=1_000_000
        ),
    )(own, low, high, *fine, *weights, head, *fixed, pos, vel, where, dest, rank)


def exchange(value, count_x, count_y, rule):
    pairs = []
    for i in range(count_x):
        for j in range(count_y):
            a, b = rule(i, j)
            pairs.append((i * count_y + j, (a % count_x) * count_y + b % count_y))
    return lax.ppermute(value, ("gx", "gy"), pairs)


def body(
    position,
    velocity,
    cell_list,
    slot_weight,
    particle_cell,
    destination,
    lift,
    kernel_0a,
    kernel_1a,
    kernel_2,
    kernel_1b,
    kernel_0b,
    head,
):
    count_x, count_y = lax.axis_size("gx"), lax.axis_size("gy")
    first_core = lax.rem(lax.axis_index("gx"), 2) == 0

    def mate(value):
        return exchange(value, count_x, count_y, lambda i, j: (i ^ 1, j))

    def cross(value):
        return exchange(value, count_x, count_y, lambda i, j: (i + 1 if i % 2 else i - 1, j))

    def along_y(value):
        return exchange(value, count_x, count_y, lambda i, j: (i, j - 1 if i % 2 else j + 1))

    def along(value, step):
        return exchange(value, count_x, count_y, lambda i, j: (i, j + step))

    def either(if_first, if_second):
        return jnp.where(first_core, if_first, if_second)

    def cat(parts, axis):
        return jnp.concatenate(parts, axis=axis)

    def barrier(*values):
        return lax.optimization_barrier(values)

    fixed = constants()
    dest = destination.reshape(16, 128)

    raw = (kernel_0a, lift.T, kernel_1a, kernel_2, kernel_1b, kernel_0b, dest)
    mine, *raw = deposit(velocity, cell_list, slot_weight, raw)
    kernel_0a, lifting, kernel_1a, kernel_2, kernel_1b, kernel_0b, dest = raw
    theirs = mate(mine)
    (w0a,) = in_vmem(first_kernel, [((768, 512), bf16)], (lifting, kernel_0a))
    theirs, w0a = barrier(theirs, w0a)
    near = cross(cat([mine, either(theirs[0:1], theirs[1:2])], 0))
    chip = cat([either(mine, theirs), either(theirs, mine)], 0)

    w1a, w2 = in_vmem(
        middle_kernel,
        [((9, 256, 256), bf16), ((9, 128, 128), bf16)],
        (kernel_1a, kernel_2),
        (theirs,),
    )
    near, w1a, w2 = barrier(near, w1a, w2)
    far = mate(near)
    left, right = either(near, far), either(far, near)
    wide = cat([left[2:3], left[0:2], chip, right], 0)
    near = along_y(
        either(
            cat([wide[:, 10:16], wide[:, 26:32]], 1), cat([wide[:, 0:6], wide[:, 16:22]], 1)
        )
    )
    own = either(wide[0:8], wide[2:10])
    fine = own_part(own, w0a, fixed[0])
    w1b, w0b, headed, rank = in_vmem(
        last_kernel,
        [((9, 256, 256), bf16), ((9, 512, 512), bf16), ((512, 128), bf16), ((16, 128), i32)],
        (head, dest, kernel_1b, kernel_0b),
        (own,),
    )
    weights = (w0a, w1a, w2, w1b, w0b)
    near, fine, weights, headed, rank = barrier(near, fine, weights, headed, rank)
    far = mate(either(near[2:10], near[0:8]))
    near = either(near[0:8], near[2:10])
    low, high = either(near, far), either(far, near)

    packed = network(
        own,
        low,
        high,
        fine,
        weights,
        headed,
        fixed,
        position.reshape(3, 16, 128),
        velocity.reshape(3, 16, 128),
        particle_cell.reshape(16, 128),
        dest,
        rank,
    )

    behind, level, ahead = packed[0:72], packed[72:144], packed[144:216]
    from_cross = cross(either(behind, ahead))
    from_mate = mate(either(ahead, behind))
    behind = either(from_mate, from_cross)
    ahead = either(from_cross, from_mate)
    groups = (behind, level, ahead)
    down = cat([group[0:24] for group in groups], 0)
    upward = cat([group[48:72] for group in groups], 0)
    upward, down = along(upward, 1), along(down, -1)
    blocks = []
    for a in range(3):
        blocks.append(down[24 * a : 24 * a + 24])
        blocks.append(groups[a][24:48])
        blocks.append(upward[24 * a : 24 * a + 24])
    inbox = jnp.stack(blocks, axis=0).reshape(9, 6, CAP)
    return inbox.astype(f32).transpose(1, 0, 2).reshape(6, 9 * CAP)


def solution(mesh):
    in_specs = (
        P(None, ("gx", "gy")),
        P(None, ("gx", "gy")),
        P(None, "gx", "gy", None),
        P(None, "gx", "gy", None),
        P(("gx", "gy")),
        P(("gx", "gy"), None),
        P(),
        P(),
        P(),
        P(),
        P(),
        P(),
        P(),
    )
    out_specs = P(None, ("gx", "gy"))
    return jax.shard_map(body, mesh=mesh, in_specs=in_specs, out_specs=out_specs, check_vma=False)
```
